32 devices in a mesh: group: 2 (over y), expert: 4 (over z), dp: 2 (over x), sub: 2 (over core).
Axes of the slice: x: 2, y: 2, z: 4, core: 2. Of those that a mesh axis runs over, the one named last changes fastest.
Arguments:
- layer_input: bfloat16 [1024, 2048], P(('group', 'expert', 'dp', 'sub')), parts along dimension 0, may hold values from -6 to 6
- output_grad: bfloat16 [1024, 2048], P(('group', 'expert', 'dp', 'sub')), parts along dimension 0, may hold values from -6 to 6
- routes: int32 [1024, 8], P(('group', 'expert', 'dp', 'sub')), parts along dimension 0, may hold values from 0 to 7, as said below
- routing_weight: float32 [1024, 8], P(('group', 'expert', 'dp', 'sub')), parts along dimension 0, may hold values from 0.02 to 0.5
- gate_proj: bfloat16 [8, 2048, 768], P(('expert', 'dp'), None, 'sub'), may hold values from -0.125 to 0.125
- up_proj: bfloat16 [8, 2048, 768], P(('expert', 'dp'), None, 'sub'), may hold values from -0.125 to 0.125
- down_proj: bfloat16 [8, 768, 2048], P(('expert', 'dp'), 'sub'), may hold values from -0.21875 to 0.21875
Outputs:
- input_grad: bfloat16 [1024, 2048], P(('group', 'expert', 'dp', 'sub')), parts along dimension 0
- routing_grad: float32 [1024, 8], P(('group', 'expert', 'dp', 'sub')), parts along dimension 0
- gate_grads: bfloat16 [16, 2048, 768], P(('group', 'expert', 'dp'), None, 'sub'), parts along dimension 0
- up_grads: bfloat16 [16, 2048, 768], P(('group', 'expert', 'dp'), None, 'sub'), parts along dimension 0
- down_grads: bfloat16 [16, 768, 2048], P(('group', 'expert', 'dp'), 'sub'), parts along dimension 0
The draws below stay inside these ranges and needn't reach their ends.
There are 2 independent parts, one for each index of `group`. The reference program is written for one: setup_inputs(seed, part) draws one part's arguments, and reference() takes and returns one part's arrays. A program takes and returns all parts, laid end to end along the dimension named above; an argument that names none is the same for every part. Nothing has to cross between parts.
Inputs may be any that keep to these rules, and one draw needn't show every extreme that they name: `routes`: the expert numbers form 8 groups of 1 consecutive numbers, and each token names exactly one expert of every group, in any order. The tokens of one device name each expert at most 32 times; in every group one expert, the same on all devices of a part, is named exactly 32 times by the tokens of every device.
All inputs are finite; a program needn't handle non-finite values.
Results may differ from the reference program's by a relative error of at most 0.0064.
Values may be sent and summed in bfloat16 or wider, within the bound.
No kernel may reach another device: no remote copies, remote signals or barrier semaphores. Data moves between devices by JAX's collectives and lax.ppermute only.
A program may use at most 128 MiB of HBM per device.

```python
import math
import jax
import jax.numpy as jnp
from jax import lax

D = 2048
FF = 768
TOPK = 8
TOK_DEV = 32
EXPERTS = 8
MOST = 32
TOKENS = 512


def draw_routes(key, part):
    key = jax.random.fold_in(key, 17)
    group_size = EXPERTS // TOPK
    others = max(group_size - 1, 1)
    blocks = TOKENS // TOK_DEV
    pair_count = blocks * TOPK
    key_hot, key_other, key_tokens, key_order = jax.random.split(key, 4)
    hot_label = jax.random.randint(key_hot, (TOPK,), 0, group_size)
    other_perm = jax.vmap(lambda subkey: jax.random.permutation(subkey, others))(jax.random.split(key_other, pair_count)).reshape(blocks, TOPK, others)
    token_perm = jax.vmap(lambda subkey: jax.random.permutation(subkey, TOK_DEV))(jax.random.split(key_tokens, pair_count)).reshape(blocks, TOPK, TOK_DEV)
    places = jnp.arange(TOK_DEV, dtype=jnp.int32)
    cycle_index = jnp.maximum(places - MOST, 0) % others
    other_label = (hot_label[None, :, None] + 1 + other_perm[:, :, cycle_index]) % group_size
    labels = jnp.where(places[None, None, :] < MOST, hot_label[None, :, None], other_label)
    shuffled = jnp.take_along_axis(labels, token_perm, axis=2)
    expert_ids = shuffled + (jnp.arange(TOPK, dtype=jnp.int32) * group_size)[None, :, None]
    ordered = jnp.transpose(expert_ids, (0, 2, 1)).reshape(TOKENS, TOPK).astype(jnp.int32)
    column_perm = jax.vmap(lambda subkey: jax.random.permutation(subkey, TOPK))(jax.random.split(key_order, TOKENS)).astype(jnp.int32)
    return jnp.take_along_axis(ordered, column_perm, axis=1).astype(jnp.int32)


def levels(own_key, dims, pieces, low, largest):
    loudness, own = 1.0, jax.random.fold_in(own_key, 6)
    for position, blocks in pieces:
        heights = jnp.exp(jax.random.uniform(jax.random.fold_in(own, position), (blocks,), jnp.float32, low / len(pieces), largest / len(pieces)))
        loudness = loudness * jnp.repeat(heights, dims[position] // blocks).reshape([-1 if axis == position else 1 for axis in range(len(dims))])
    return loudness


def normal_values(stream_key, shape, width, reach, shards=(), kind=jnp.bfloat16):
    level = levels(stream_key, shape, shards, -0.22, 0.18) if shards else 1.0
    result = jax.random.normal(stream_key, shape, jnp.float32) * width * level
    return jnp.minimum(jnp.maximum(result, -reach), reach).astype(kind)


def setup_inputs(seed: int = 0, part: int = 0) -> dict:
    arg_keys = jax.random.split(jax.random.key(seed), 8)
    part_splits = jax.random.split(jax.random.fold_in(arg_keys[7], part), 8)
    layer_input = normal_values(part_splits[0], (TOKENS, D), 1.0, 6.0, ((0, 16),))
    output_grad = normal_values(part_splits[1], (TOKENS, D), 1.0, 6.0, ((0, 16),))
    routes = draw_routes(jax.random.fold_in(jax.random.fold_in(arg_keys[7], part), 71), part)
    routing_weight = jnp.clip(jnp.exp(math.log(0.5) - 3.218876 * jax.random.uniform(part_splits[3], (TOKENS, TOPK), jnp.float32) ** levels(part_splits[3], (TOKENS, TOPK), ((0, 16),), -0.2, 0.2)), 0.02, 0.5)
    gate_proj = normal_values(arg_keys[4], (EXPERTS, D, FF), D ** -0.5, 0.125, ((0, 8), (2, 2)))
    up_proj = normal_values(arg_keys[5], (EXPERTS, D, FF), D ** -0.5, 0.125, ((0, 8), (2, 2)))
    down_proj = normal_values(arg_keys[6], (EXPERTS, FF, D), FF ** -0.5, 0.21875, ((0, 8), (1, 2)))
    return {"layer_input": layer_input, "output_grad": output_grad, "routes": routes, "routing_weight": routing_weight, "gate_proj": gate_proj, "up_proj": up_proj, "down_proj": down_proj}


def reference(layer_input, output_grad, routes, routing_weight, gate_proj, up_proj, down_proj):
    tokens, model_width = layer_input.shape
    top_count = routes.shape[1]
    experts, _, hidden = gate_proj.shape
    row_total = tokens * top_count
    flat_ids = routes.reshape(-1).astype(jnp.int32)
    sorted_rows = jnp.argsort(flat_ids, stable=True).astype(jnp.int32)
    member = (flat_ids[:, None] == jnp.arange(experts, dtype=jnp.int32)[None, :]).astype(jnp.int32)
    counts = jnp.sum(member, axis=0).astype(jnp.int32)
    starts = (jnp.cumsum(counts) - counts).astype(jnp.int32)
    block_rows = 128

    def per_expert(scan_carry, expert):
        gate_w = gate_proj[expert]
        up_w = up_proj[expert]
        down_w = down_proj[expert]

        def step(block_index, loop_state):
            acc_input, acc_route, grad_gate, grad_up, grad_down = loop_state
            place_index = starts[expert] + block_index * block_rows + jnp.arange(block_rows, dtype=jnp.int32)
            valid = place_index < starts[expert] + counts[expert]
            row_ids = sorted_rows[jnp.minimum(place_index, row_total - 1)]
            token_index = (row_ids // top_count).astype(jnp.int32)
            pick_slot = (row_ids % top_count).astype(jnp.int32)
            weight_now = routing_weight[token_index, pick_slot]
            row_scale = jnp.where(valid, weight_now, jnp.zeros((), routing_weight.dtype))
            rows_x = jnp.where(valid[:, None], layer_input[token_index], jnp.zeros((), layer_input.dtype))
            rows_e = (row_scale[:, None] * output_grad[token_index].astype(jnp.float32)).astype(jnp.bfloat16)
            pre_gate = jnp.dot(rows_x, gate_w, preferred_element_type=jnp.float32)
            pre_up = jnp.dot(rows_x, up_w, preferred_element_type=jnp.float32)
            sigmoid_gate = jax.nn.sigmoid(pre_gate)
            silu_gate = pre_gate * sigmoid_gate
            hidden_act = silu_gate * pre_up
            hidden_low = hidden_act.astype(jnp.bfloat16)
            back_hidden = jnp.dot(rows_e, down_w.T, preferred_element_type=jnp.float32)
            product = jnp.sum(hidden_act * back_hidden, axis=1).astype(jnp.bfloat16)
            silu_slope = sigmoid_gate * (1.0 + pre_gate * (1.0 - sigmoid_gate))
            diff_gate = (back_hidden * pre_up * silu_slope).astype(jnp.bfloat16)
            diff_up = (back_hidden * silu_gate).astype(jnp.bfloat16)
            row_grad = jnp.dot(diff_gate, gate_w.T, preferred_element_type=jnp.float32) + jnp.dot(diff_up, up_w.T, preferred_element_type=jnp.float32)
            row_low = row_grad.astype(jnp.bfloat16).astype(jnp.float32)
            acc_input = acc_input.at[token_index].add(jnp.where(valid[:, None], row_low, jnp.zeros((), jnp.float32)))
            route_term = product.astype(jnp.float32) / weight_now
            acc_route = acc_route.at[token_index, pick_slot].add(jnp.where(valid, route_term, jnp.zeros((), jnp.float32)))
            grad_gate = grad_gate + jnp.dot(rows_x.T, diff_gate, preferred_element_type=jnp.float32)
            grad_up = grad_up + jnp.dot(rows_x.T, diff_up, preferred_element_type=jnp.float32)
            grad_down = grad_down + jnp.dot(hidden_low.T, rows_e, preferred_element_type=jnp.float32)
            return (acc_input, acc_route, grad_gate, grad_up, grad_down)

        start_state = (scan_carry[0], scan_carry[1], jnp.zeros((model_width, hidden), jnp.float32), jnp.zeros((model_width, hidden), jnp.float32), jnp.zeros((hidden, model_width), jnp.float32))
        block_total = (counts[expert] + block_rows - 1) // block_rows
        acc_input, acc_route, grad_gate, grad_up, grad_down = lax.fori_loop(0, block_total, step, start_state)
        return (acc_input, acc_route), (grad_gate.astype(jnp.bfloat16), grad_up.astype(jnp.bfloat16), grad_down.astype(jnp.bfloat16))

    start_carry = (jnp.zeros((tokens, model_width), jnp.float32), jnp.zeros((tokens, top_count), jnp.float32))
    final_carry, grads = lax.scan(per_expert, start_carry, jnp.arange(experts, dtype=jnp.int32))
    return (final_carry[0].astype(jnp.bfloat16), final_carry[1], grads[0], grads[1], grads[2])
```

```python
import functools

import jax
import jax.numpy as jnp
from jax import lax
from jax.experimental import pallas as pl
from jax.experimental.pallas import tpu as pltpu
from jax.sharding import PartitionSpec as P

F32 = jnp.float32
BF16 = jnp.bfloat16
SIDE = 128
NT = (((1,), (1,)), ((), ()))
TN = (((0,), (0,)), ((), ()))
VMEM_LIMIT = 40 * 1024 * 1024


def whole(shape):
    return pl.BlockSpec(shape, lambda *_: (0,) * len(shape))


def split_columns(values, count, lane):
    high = values.astype(BF16)
    low = (values - high.astype(F32)).astype(BF16)
    zero = jnp.zeros_like(high)
    return jnp.where(lane < count, high, jnp.where(lane < 2 * count, low, zero))


def pack_kernel(x_ref, e_ref, routes_ref, weight_ref, out_ref):
    tok_count, width = x_ref.shape
    top_count = routes_ref.shape[1]
    out_ref[:tok_count, :width] = x_ref[...]
    out_ref[tok_count:, :width] = e_ref[...]
    routes = routes_ref[...]
    weight = weight_ref[...]
    lane = lax.broadcasted_iota(jnp.int32, (tok_count, SIDE), 1)
    expert = lax.rem(lane, top_count)
    table = jnp.zeros((tok_count, SIDE), F32)
    for k in range(top_count):
        table += jnp.where(routes[:, k : k + 1] == expert, weight[:, k : k + 1], 0.0)
    out_ref[:tok_count, width:] = split_columns(table, top_count, lane)
    out_ref[tok_count:, width:] = jnp.zeros((tok_count, SIDE), BF16)


def pack(x, e, routes, weight):
    tok_count, width = x.shape
    return pl.pallas_call(
        pack_kernel,
        out_shape=jax.ShapeDtypeStruct((2 * tok_count, width + SIDE), BF16),
        name="pack_tokens",
    )(x, e, routes, weight)


def rows_kernel(shards, steps, expert_ref, *refs):
    shard_refs = refs[:shards]
    gate_a, gate_b, up_a, up_b, down_a, down_b = refs[shards : shards + 6]
    keep_ref, send_ref, xe_ref, own_ref, other_ref, weight_ref, total_ref, product_ref = refs[shards + 6 :]
    step = pl.program_id(0)
    tok_count = shard_refs[0].shape[0] // 2
    rows = shards * tok_count
    half = rows // 2
    width = xe_ref.shape[1]
    experts = expert_ref[1]

    @pl.when(step == 0)
    def _():
        lane = lax.broadcasted_iota(jnp.int32, (tok_count, SIDE), 1)
        wanted = (lane == expert_ref[0]) | (lane == expert_ref[0] + experts)
        for i, ref in enumerate(shard_refs):
            here = slice(i * tok_count, (i + 1) * tok_count)
            xe_ref[here, :] = ref[:tok_count, :width]
            xe_ref[rows + i * tok_count : rows + (i + 1) * tok_count, :] = ref[tok_count:, :width]
            table = ref[:tok_count, width:].astype(F32)
            weight_ref[here, :] = jnp.sum(jnp.where(wanted, table, 0.0), axis=1, keepdims=True)

    x = xe_ref[:rows, :]
    e = xe_ref[rows:, :]
    block = gate_a.shape[-1]
    gate_w = jnp.concatenate([gate_a[0], gate_b[0]], axis=1)
    up_w = jnp.concatenate([up_a[0], up_b[0]], axis=1)
    down_w = jnp.concatenate([down_a[0], down_b[0]], axis=0)
    pre_gate = jnp.dot(x, gate_w, preferred_element_type=F32)
    pre_up = jnp.dot(x, up_w, preferred_element_type=F32)
    back = lax.dot_general(e, down_w, NT, preferred_element_type=F32)
    sig = jax.nn.sigmoid(pre_gate)
    silu = pre_gate * sig
    hidden = silu * pre_up
    product = jnp.sum(hidden * back, axis=1, keepdims=True)
    weight = weight_ref[...]
    scaled_back = back * weight
    diff_gate = (scaled_back * pre_up * (sig * (1.0 + pre_gate * (1.0 - sig)))).astype(BF16)
    diff_up = (scaled_back * silu).astype(BF16)
    hidden_low = (hidden * weight).astype(BF16)
    for i, ref in enumerate((own_ref, other_ref)):
        here = slice(i * block, (i + 1) * block)
        ref[:, :block] = diff_gate[:, here]
        ref[:, block : 2 * block] = diff_up[:, here]
        ref[:, 2 * block :] = hidden_low[:, here]
    part = lax.dot_general(diff_gate, gate_w, NT, preferred_element_type=F32) + lax.dot_general(
        diff_up, up_w, NT, preferred_element_type=F32
    )

    @pl.when(step == 0)
    def _():
        total_ref[...] = part
        product_ref[...] = product

    @pl.when(step > 0)
    def _():
        total_ref[...] += part
        product_ref[...] += product

    @pl.when(step == steps - 1)
    def _():
        lane = lax.broadcasted_iota(jnp.int32, (rows, SIDE), 1)
        place = lax.rem(lane, experts) == expert_ref[0]
        side = split_columns(jnp.where(place, product_ref[...], 0.0), experts, lane)
        keep_ref[:, :width] = total_ref[:half, :]
        keep_ref[:, width:] = side[:half].astype(F32)
        send_ref[:, :width] = total_ref[half:, :].astype(BF16)
        send_ref[:, width:] = side[half:]


def expert_rows_chunk(name, shards, expert_info, weights):
    count = len(shards)
    tok_count = shards[0].shape[0] // 2
    wide = shards[0].shape[1]
    width = wide - SIDE
    rows = count * tok_count
    half_hidden = weights[0].shape[2]
    block = 128
    steps = half_hidden // block
    column = pl.BlockSpec((1, width, block), lambda j: (0, 0, j))
    row = pl.BlockSpec((1, block, width), lambda j: (0, j, 0))
    flops = 5 * 2 * rows * width * 2 * half_hidden
    return pl.pallas_call(
        functools.partial(rows_kernel, count, steps),
        grid=(steps,),
        in_specs=[pl.BlockSpec(memory_space=pltpu.SMEM)]
        + [whole(shards[0].shape)] * count
        + [column, column, column, column, row, row],
        out_specs=[
            whole((rows // 2, wide)),
            whole((rows // 2, wide)),
            whole((2 * rows, width)),
            pl.BlockSpec((rows, 3 * block), lambda j: (0, j)),
            pl.BlockSpec((rows, 3 * block), lambda j: (0, j)),
        ],
        out_shape=[
            jax.ShapeDtypeStruct((rows // 2, wide), F32),
            jax.ShapeDtypeStruct((rows // 2, wide), BF16),
            jax.ShapeDtypeStruct((2 * rows, width), BF16),
            jax.ShapeDtypeStruct((rows, 3 * half_hidden), BF16),
            jax.ShapeDtypeStruct((rows, 3 * half_hidden), BF16),
        ],
        scratch_shapes=[
            pltpu.VMEM((rows, 1), F32),
            pltpu.VMEM((rows, width), F32),
            pltpu.VMEM((rows, 1), F32),
        ],
        compiler_params=pltpu.CompilerParams(vmem_limit_bytes=VMEM_LIMIT),
        cost_estimate=pl.CostEstimate(
            flops=flops, bytes_accessed=12 * width * half_hidden + 20 * rows * width, transcendentals=rows * half_hidden * 2
        ),
        name=name,
    )(expert_info, *shards, *weights)


def grads_kernel(parts, steps, *refs):
    x_refs = refs[:parts]
    e_refs = refs[parts : 2 * parts]
    diff_refs = refs[2 * parts : 3 * parts]
    gate_ref, up_ref, down_ref, diffs, hidden_t = refs[3 * parts :]
    block = 128
    hidden = gate_ref.shape[2]

    @pl.when(pl.program_id(0) == 0)
    def _():
        start = 0
        lows = []
        for ref in diff_refs:
            rows = ref.shape[0]
            for j in range(hidden // block):
                base = 3 * block * j
                diffs[start : start + rows, j * block : (j + 1) * block] = ref[:, base : base + block]
                diffs[start : start + rows, hidden + j * block : hidden + (j + 1) * block] = ref[
                    :, base + block : base + 2 * block
                ]
            lows.append(
                jnp.concatenate(
                    [ref[:, 3 * block * j + 2 * block : 3 * block * (j + 1)] for j in range(hidden // block)], axis=1
                )
            )
            start += rows
        hidden_t[...] = jnp.concatenate(lows, axis=0).T

    x = jnp.concatenate([ref[...] for ref in x_refs], axis=0)
    e = jnp.concatenate([ref[...] for ref in e_refs], axis=0)
    both = lax.dot_general(x, diffs[...], TN, preferred_element_type=F32).astype(BF16)
    gate_ref[0] = both[:, :hidden]
    up_ref[0] = both[:, hidden:]
    down_ref[0] = jnp.dot(hidden_t[...], e, preferred_element_type=F32).astype(BF16)


def weight_grads(xe_parts, diff_parts):
    count = len(xe_parts)
    width = xe_parts[0].shape[1]
    hidden = diff_parts[0].shape[1] // 3
    total = sum(part.shape[0] for part in diff_parts)
    block = 256
    steps = width // block
    x_specs = [pl.BlockSpec((part.shape[0] // 2, block), lambda i: (0, i)) for part in xe_parts]
    e_specs = [pl.BlockSpec((part.shape[0] // 2, block), lambda i: (1, i)) for part in xe_parts]
    return pl.pallas_call(
        functools.partial(grads_kernel, count, steps),
        grid=(steps,),
        in_specs=x_specs + e_specs + [whole(part.shape) for part in diff_parts],
        out_specs=[
            pl.BlockSpec((1, block, hidden), lambda i: (0, i, 0)),
            pl.BlockSpec((1, block, hidden), lambda i: (0, i, 0)),
            pl.BlockSpec((1, hidden, block), lambda i: (0, 0, i)),
        ],
        out_shape=[
            jax.ShapeDtypeStruct((1, width, hidden), BF16),
            jax.ShapeDtypeStruct((1, width, hidden), BF16),
            jax.ShapeDtypeStruct((1, hidden, width), BF16),
        ],
        scratch_shapes=[pltpu.VMEM((total, 2 * hidden), BF16), pltpu.VMEM((hidden, total), BF16)],
        compiler_params=pltpu.CompilerParams(vmem_limit_bytes=VMEM_LIMIT),
        cost_estimate=pl.CostEstimate(
            flops=6 * total * width * hidden, bytes_accessed=4 * total * width + 6 * width * hidden, transcendentals=0
        ),
        name="weight_grads",
    )(*xe_parts, *xe_parts, *diff_parts)


def swap(value, axis):
    return lax.ppermute(value, axis, [(0, 1), (1, 0)])


def far(value, axis, distance):
    return lax.ppermute(value, axis, [(i, i ^ distance) for i in range(lax.axis_size(axis))])


def every_token_to_every_expert(
    layer_input, output_grad, routes, routing_weight, gate_proj, up_proj, down_proj
):
    tok_count, width = layer_input.shape
    top_count = routes.shape[1]
    lines = lax.axis_size("expert")
    expert = lax.axis_index("expert") * lax.axis_size("dp") + lax.axis_index("dp")
    expert_info = jnp.stack([expert, jnp.int32(top_count)]).astype(jnp.int32)
    packed = pack(layer_input, output_grad, routes, routing_weight)
    order = [k for k in range(1, lines) if k != 1] + [1] if lines > 1 else []
    columns = {0: packed}
    for k in order:
        columns[k] = far(packed, "expert", k)
    across = {k: swap(columns[k], "dp") for k in range(lines)}
    other_weights = [swap(array, "sub") for array in (gate_proj, up_proj, down_proj)]
    weights = (gate_proj, other_weights[0], up_proj, other_weights[1], down_proj, other_weights[2])
    last = lines - 1
    chunks = [list(range(last)), [last]] if lines > 1 else [[0]]
    own_sum = None
    arrived = []
    xe_parts, diff_parts = [], []
    for number, chunk in enumerate(chunks):
        shards = [columns[k] for k in chunk] + [across[k] for k in chunk]
        keep, send, xe, own_diff, other_diff = expert_rows_chunk("rows_%d" % number, shards, expert_info, weights)
        summed = keep + swap(send, "dp").astype(F32)
        for i, k in enumerate(chunk):
            block = summed[i * tok_count : (i + 1) * tok_count]
            if k == 0:
                own_sum = block
            else:
                arrived.append(far(block.astype(BF16), "expert", k))
        xe_parts += [xe, swap(xe, "sub")]
        diff_parts += [own_diff, swap(other_diff, "sub")]
    total = own_sum
    for block in arrived:
        total = total + block.astype(F32)
    input_grad = total[:, :width].astype(BF16)
    products = total[:, width : width + top_count] + total[:, width + top_count : width + 2 * top_count]
    chosen = routes[:, :, None] == jnp.arange(top_count, dtype=jnp.int32)[None, None, :]
    routing_grad = jnp.sum(jnp.where(chosen, products[:, None, :], 0.0), axis=2)
    gate_grads, up_grads, down_grads = weight_grads(xe_parts, diff_parts)
    return (input_grad, routing_grad, gate_grads, up_grads, down_grads)


def expert_rows(inputs, gate_w, up_w, down_w):
    rows_x, rows_e = inputs
    leading = rows_x.shape[:-1]
    model_width = rows_x.shape[-1]
    hidden = gate_w.shape[1]
    flat_x = rows_x.reshape(-1, model_width)
    flat_e = rows_e.reshape(-1, model_width)
    contract = (((1,), (1,)), ((), ()))
    pre_gate = jnp.dot(flat_x, gate_w, preferred_element_type=jnp.float32)
    pre_up = jnp.dot(flat_x, up_w, preferred_element_type=jnp.float32)
    sigmoid_gate = jax.nn.sigmoid(pre_gate)
    silu_gate = pre_gate * sigmoid_gate
    hidden_act = silu_gate * pre_up
    hidden_low = hidden_act.astype(jnp.bfloat16)
    back_hidden = lax.dot_general(flat_e, down_w, contract, preferred_element_type=jnp.float32)
    product = jnp.sum(hidden_act * back_hidden, axis=1)
    silu_slope = sigmoid_gate * (1.0 + pre_gate * (1.0 - sigmoid_gate))
    diff_gate = (back_hidden * pre_up * silu_slope).astype(jnp.bfloat16)
    diff_up = (back_hidden * silu_gate).astype(jnp.bfloat16)
    row_grad = lax.dot_general(
        diff_gate, gate_w, contract, preferred_element_type=jnp.float32
    ) + lax.dot_general(diff_up, up_w, contract, preferred_element_type=jnp.float32)
    return (
        row_grad.reshape(leading + (model_width,)),
        product.reshape(leading),
        rows_x,
        rows_e,
        hidden_low.reshape(leading + (hidden,)),
        diff_gate.reshape(leading + (hidden,)),
        diff_up.reshape(leading + (hidden,)),
    )


def chosen_experts(layer_input, output_grad, routes, routing_weight, gate_proj, up_proj, down_proj):
    tok_count, model_width = layer_input.shape
    top_count = routes.shape[1]
    positions = lax.axis_size(("expert", "dp"))
    capacity = min(tok_count, 2 * tok_count * top_count // positions)
    row_count = tok_count * top_count
    slot_count = positions * capacity
    target = routes.reshape(-1)
    member = (target[:, None] == jnp.arange(positions, dtype=jnp.int32)[None, :]).astype(jnp.int32)
    earlier = jnp.cumsum(member, axis=0) - member
    slot_rank = jnp.sum(earlier * member, axis=1)
    slot_index = target * capacity + slot_rank
    source = (
        jnp.full((slot_count,), row_count, jnp.int32)
        .at[slot_index]
        .set(jnp.arange(row_count, dtype=jnp.int32))
    )
    filled = source < row_count
    picked = jnp.minimum(source, row_count - 1)
    token_index = picked // top_count
    row_scale = jnp.where(filled, routing_weight.reshape(-1)[picked], 0.0)
    send_x = jnp.where(
        filled[:, None], layer_input[token_index], jnp.zeros((), layer_input.dtype)
    ).reshape(positions, 1, capacity, model_width)
    send_e = (
        (row_scale[:, None] * output_grad[token_index].astype(jnp.float32))
        .astype(jnp.bfloat16)
        .reshape(positions, 1, capacity, model_width)
    )
    gate_w = gate_proj[0]
    up_w = up_proj[0]
    down_w = down_proj[0]
    hidden = gate_w.shape[1]
    paired = (
        lax.all_gather(send_x, "sub", axis=1, tiled=True),
        lax.all_gather(send_e, "sub", axis=1, tiled=True),
    )
    results = expert_rows(
        (
            lax.all_to_all(paired[0], ("expert", "dp"), split_axis=0, concat_axis=0, tiled=True),
            lax.all_to_all(paired[1], ("expert", "dp"), split_axis=0, concat_axis=0, tiled=True),
        ),
        gate_w,
        up_w,
        down_w,
    )
    row_part, product_part, rows_x, rows_e, hidden_low, diff_gate, diff_up = results
    returned = (
        lax.all_to_all(row_part, ("expert", "dp"), split_axis=0, concat_axis=0, tiled=True),
        lax.all_to_all(product_part, ("expert", "dp"), split_axis=0, concat_axis=0, tiled=True),
    )
    summed = (
        lax.psum_scatter(returned[0], "sub", scatter_dimension=1, tiled=True),
        lax.psum_scatter(returned[1], "sub", scatter_dimension=1, tiled=True),
    )
    back_rows = summed[0].astype(jnp.bfloat16)
    back_products = summed[1].astype(jnp.bfloat16)
    per_row = (
        back_rows.reshape(slot_count, model_width)[slot_index]
        .astype(jnp.float32)
        .reshape(tok_count, top_count, model_width)
    )
    input_grad = jnp.sum(per_row, axis=1).astype(jnp.bfloat16)
    routing_grad = (
        back_products.reshape(slot_count)[slot_index]
        .astype(jnp.float32)
        .reshape(tok_count, top_count)
        / routing_weight
    )
    over_rows = (((0,), (0,)), ((), ()))
    flat_x = rows_x.reshape(-1, model_width)
    flat_e = rows_e.reshape(-1, model_width)
    gate_grads = lax.dot_general(
        flat_x, diff_gate.reshape(-1, hidden), over_rows, preferred_element_type=jnp.float32
    ).astype(jnp.bfloat16)[None]
    up_grads = lax.dot_general(
        flat_x, diff_up.reshape(-1, hidden), over_rows, preferred_element_type=jnp.float32
    ).astype(jnp.bfloat16)[None]
    down_grads = lax.dot_general(
        hidden_low.reshape(-1, hidden), flat_e, over_rows, preferred_element_type=jnp.float32
    ).astype(jnp.bfloat16)[None]
    return (input_grad, routing_grad, gate_grads, up_grads, down_grads)


def per_device(layer_input, output_grad, routes, routing_weight, gate_proj, up_proj, down_proj):
    args = (layer_input, output_grad, routes, routing_weight, gate_proj, up_proj, down_proj)
    lines = lax.axis_size("expert")
    pairs = lax.axis_size("dp") == 2 and lax.axis_size("sub") == 2 and lines & (lines - 1) == 0
    if pairs and 2 * lines == routes.shape[1] and gate_proj.shape[0] == 1:
        return every_token_to_every_expert(*args)
    return chosen_experts(*args)


def solution(mesh):
    placed = (
        P(("group", "expert", "dp", "sub"), None),
        P(("group", "expert", "dp", "sub"), None),
        P(("group", "expert", "dp", "sub"), None),
        P(("group", "expert", "dp", "sub"), None),
        P(("expert", "dp"), None, "sub"),
        P(("expert", "dp"), None, "sub"),
        P(("expert", "dp"), "sub", None),
    )
    return jax.shard_map(
        per_device,
        mesh=mesh,
        in_specs=placed,
        out_specs=(
            P(("group", "expert", "dp", "sub"), None),
            P(("group", "expert", "dp", "sub"), None),
            P(("group", "expert", "dp"), None, "sub"),
            P(("group", "expert", "dp"), None, "sub"),
            P(("group", "expert", "dp"), "sub", None),
        ),
        check_vma=False,
    )
```

```python
import functools

import jax
import jax.numpy as jnp
from jax import lax
from jax.experimental import pallas as pl
from jax.experimental.pallas import tpu as pltpu
from jax.sharding import PartitionSpec as P

F32 = jnp.float32
BF16 = jnp.bfloat16
SIDE = 128
NT = (((1,), (1,)), ((), ()))
TN = (((0,), (0,)), ((), ()))
MIB = 1024 * 1024


def split_columns(values, count, lane):
    high = values.astype(BF16)
    low = (values - high.astype(F32)).astype(BF16)
    zero = jnp.zeros_like(high)
    return jnp.where(lane < count, high, jnp.where(lane < 2 * count, low, zero))


def in_vmem(count):
    return [pl.BlockSpec(memory_space=pltpu.VMEM)] * count


def in_hbm(count):
    return [pl.BlockSpec(memory_space=pl.ANY)] * count


def held(*arrays):
    return [pltpu.with_memory_space_constraint(array, pltpu.VMEM) for array in arrays]


def left(*arrays):
    return [pltpu.with_memory_space_constraint(array, pltpu.HBM) for array in arrays]


def pack_kernel(x_ref, e_ref, routes_ref, weight_ref, out_ref, routes_held, weight_held, sems):
    tok_count, width = x_ref.shape
    top_count = routes_ref.shape[0]
    copies = [
        pltpu.make_async_copy(routes_ref, routes_held, sems.at[0]),
        pltpu.make_async_copy(weight_ref, weight_held, sems.at[1]),
        pltpu.make_async_copy(x_ref, out_ref.at[pl.ds(0, tok_count), pl.ds(0, width)], sems.at[2]),
        pltpu.make_async_copy(e_ref, out_ref.at[pl.ds(tok_count, tok_count), pl.ds(0, width)], sems.at[3]),
    ]
    for copy in copies:
        copy.start()
    out_ref[tok_count:, width:] = jnp.zeros((tok_count, SIDE), BF16)
    lane = lax.broadcasted_iota(jnp.int32, (tok_count, SIDE), 1)
    expert = lax.rem(lax.broadcasted_iota(jnp.int32, (SIDE, tok_count), 0), top_count)
    copies[0].wait()
    copies[1].wait()
    routes = routes_held[...]
    weight = weight_held[...]
    table = jnp.zeros((SIDE, tok_count), F32)
    for k in range(top_count):
        table += jnp.where(routes[k : k + 1, :] == expert, weight[k : k + 1, :], 0.0)
    out_ref[:tok_count, width:] = split_columns(table.T, top_count, lane)
    copies[2].wait()
    copies[3].wait()


def pack(x, e, routes, weight):
    tok_count, width = x.shape
    top_count = routes.shape[1]
    return pl.pallas_call(
        pack_kernel,
        in_specs=in_hbm(4),
        out_specs=in_vmem(1)[0],
        out_shape=pltpu.VMEM((2 * tok_count, width + SIDE), BF16),
        scratch_shapes=[
            pltpu.VMEM((top_count, tok_count), jnp.int32),
            pltpu.VMEM((top_count, tok_count), F32),
            pltpu.SemaphoreType.DMA((4,)),
        ],
        compiler_params=pltpu.CompilerParams(vmem_limit_bytes=4 * MIB),
        name="pack_tokens",
    )(*left(x, e, routes.T, weight.T))


def stage_kernel(gate_ref, up_ref, wide_ref, sems):
    _, width, hidden = gate_ref.shape
    pieces = sems.shape[1]
    block = width // pieces
    copies = []
    for i in range(pieces):
        here = pl.ds(i * block, block)
        copies += [
            pltpu.make_async_copy(gate_ref.at[0, here], wide_ref.at[here, pl.ds(0, hidden)], sems.at[0, i]),
            pltpu.make_async_copy(up_ref.at[0, here], wide_ref.at[here, pl.ds(hidden, hidden)], sems.at[1, i]),
        ]
    for copy in copies:
        copy.start()
    for copy in copies:
        copy.wait()


def stage(gate_w, up_w):
    _, width, hidden = gate_w.shape
    return pl.pallas_call(
        stage_kernel,
        in_specs=in_hbm(2),
        out_specs=in_vmem(1)[0],
        out_shape=pltpu.VMEM((width, 2 * hidden), BF16),
        scratch_shapes=[pltpu.SemaphoreType.DMA((2, 4))],
        compiler_params=pltpu.CompilerParams(vmem_limit_bytes=8 * MIB),
        cost_estimate=pl.CostEstimate(flops=1, bytes_accessed=1, transcendentals=0),
        name="stage_weights",
    )(*left(gate_w, up_w))


def rows_kernel(shards, expert_ref, *refs):
    shard_refs = refs[:shards]
    wide_ref, down_ref, keep_ref, send_ref, xe_ref, diff_ref, tall_ref, table_ref, sems = refs[shards:]
    tok_count = shard_refs[0].shape[0] // 2
    rows = shards * tok_count
    half = rows // 2
    hidden, width = tall_ref.shape
    experts = expert_ref[1]
    x_copies, e_copies = [], []
    for i, ref in enumerate(shard_refs):
        here = pl.ds(i * tok_count, tok_count)
        x_copies.append((ref.at[pl.ds(0, tok_count), pl.ds(0, width)], xe_ref.at[here]))
        e_copies.append(
            (ref.at[pl.ds(tok_count, tok_count), pl.ds(0, width)], xe_ref.at[pl.ds(rows + i * tok_count, tok_count)])
        )
        e_copies.append((ref.at[pl.ds(0, tok_count), pl.ds(width, SIDE)], table_ref.at[here]))
    e_copies.append((down_ref.at[0], tall_ref))
    copies = [pltpu.make_async_copy(src, dst, sems.at[i]) for i, (src, dst) in enumerate(x_copies + e_copies)]
    for copy in copies:
        copy.start()
    lane = lax.broadcasted_iota(jnp.int32, (rows, SIDE), 1)
    wanted = (lane == expert_ref[0]) | (lane == expert_ref[0] + experts)
    for copy in copies[:shards]:
        copy.wait()
    pre = jnp.dot(xe_ref[:rows, :], wide_ref[...], preferred_element_type=F32)
    for copy in copies[shards:]:
        copy.wait()
    weight = jnp.sum(jnp.where(wanted, table_ref[...].astype(F32), 0.0), axis=1, keepdims=True)
    back = lax.dot_general(xe_ref[rows:, :], tall_ref[...], NT, preferred_element_type=F32)
    pre_gate, pre_up = pre[:, :hidden], pre[:, hidden:]
    sig = jax.nn.sigmoid(pre_gate)
    silu = pre_gate * sig
    act = silu * pre_up
    product = jnp.sum(act * back, axis=1, keepdims=True)
    back = back * weight
    diff_gate = (back * pre_up * (sig * (1.0 + pre_gate * (1.0 - sig)))).astype(BF16)
    diff_up = (back * silu).astype(BF16)
    diff = jnp.concatenate([diff_gate, diff_up], axis=1)
    diff_ref[:, : 2 * hidden] = diff
    diff_ref[:, 2 * hidden :] = (act * weight).astype(BF16)
    block = 512
    for c in range(0, width, block):
        part = lax.dot_general(diff, wide_ref[c : c + block, :], NT, preferred_element_type=F32)
        keep_ref[:, c : c + block] = part[:half]
        send_ref[:, c : c + block] = part[half:].astype(BF16)
    place = lax.rem(lane, experts) == expert_ref[0]
    side = split_columns(jnp.where(place, product, 0.0), experts, lane)
    keep_ref[:, width:] = side[:half].astype(F32)
    send_ref[:, width:] = side[half:]


def expert_rows_chunk(name, shards, expert_info, weights):
    count = len(shards)
    tok_count = shards[0].shape[0] // 2
    wide = shards[0].shape[1]
    width = wide - SIDE
    rows = count * tok_count
    hidden = weights[1].shape[1]
    return pl.pallas_call(
        functools.partial(rows_kernel, count),
        in_specs=[pl.BlockSpec(memory_space=pltpu.SMEM)] + in_hbm(count) + in_vmem(1) + in_hbm(1),
        out_specs=in_vmem(4),
        out_shape=[
            pltpu.VMEM((rows // 2, wide), F32),
            pltpu.VMEM((rows // 2, wide), BF16),
            pltpu.VMEM((2 * rows, width), BF16),
            pltpu.VMEM((rows, 3 * hidden), BF16),
        ],
        scratch_shapes=[
            pltpu.VMEM((hidden, width), BF16),
            pltpu.VMEM((rows, SIDE), BF16),
            pltpu.SemaphoreType.DMA((3 * count + 1,)),
        ],
        compiler_params=pltpu.CompilerParams(vmem_limit_bytes=16 * MIB),
        cost_estimate=pl.CostEstimate(flops=1, bytes_accessed=1, transcendentals=0),
        name=name,
    )(expert_info, *(left(*shards) if count > 4 else shards), weights[0], *left(weights[1]))


def grads_kernel(parts, first, *refs):
    xe_refs = refs[:parts]
    diff_refs = refs[parts : 2 * parts]
    gate_out, up_out, down_out, x_ref, e_ref, both_ref, down_ref, in_sems, out_sems = refs[-9:]
    hidden = gate_out.shape[2]
    span = x_ref.shape[1]
    block = span // in_sems.shape[0]
    arriving = []
    for i, c in enumerate(range(0, span, block)):
        copies = []
        start = 0
        for j, ref in enumerate(xe_refs):
            rows = ref.shape[0] // 2
            for k, dst in enumerate((x_ref, e_ref)):
                copies.append(
                    pltpu.make_async_copy(
                        ref.at[pl.ds(k * rows, rows), pl.ds(first + c, block)],
                        dst.at[pl.ds(start, rows), pl.ds(c, block)],
                        in_sems.at[i, 2 * j + k],
                    )
                )
            start += rows
        for copy in copies:
            copy.start()
        arriving.append(copies)
    diffs = jnp.concatenate([ref[:, : 2 * hidden] for ref in diff_refs], axis=0)
    hidden_t = jnp.concatenate([ref[:, 2 * hidden :] for ref in diff_refs], axis=0).T
    leaving = []
    for i, c in enumerate(range(0, span, block)):
        for copy in arriving[i]:
            copy.wait()
        here, there = pl.ds(c, block), pl.ds(first + c, block)
        both_ref[c : c + block, :] = lax.dot_general(
            x_ref[:, c : c + block], diffs, TN, preferred_element_type=F32
        ).astype(BF16)
        down_ref[:, c : c + block] = jnp.dot(
            hidden_t, e_ref[:, c : c + block], preferred_element_type=F32
        ).astype(BF16)
        copies = [
            pltpu.make_async_copy(both_ref.at[here, pl.ds(0, hidden)], gate_out.at[0, there], out_sems.at[i, 0]),
            pltpu.make_async_copy(both_ref.at[here, pl.ds(hidden, hidden)], up_out.at[0, there], out_sems.at[i, 1]),
            pltpu.make_async_copy(down_ref.at[:, here], down_out.at[0, :, there], out_sems.at[i, 2]),
        ]
        for copy in copies:
            copy.start()
        leaving += copies
    for copy in leaving:
        copy.wait()


def weight_grads(name, first, span, xe_parts, diff_parts, grads):
    count = len(xe_parts)
    width = xe_parts[0].shape[1]
    hidden = diff_parts[0].shape[1] // 3
    total = sum(part.shape[0] for part in diff_parts)
    blocks = span // 256
    return pl.pallas_call(
        functools.partial(grads_kernel, count, first),
        in_specs=in_hbm(count) + in_vmem(count) + in_hbm(len(grads)),
        out_specs=in_hbm(3),
        out_shape=[
            jax.ShapeDtypeStruct((1, width, hidden), BF16),
            jax.ShapeDtypeStruct((1, width, hidden), BF16),
            jax.ShapeDtypeStruct((1, hidden, width), BF16),
        ],
        input_output_aliases={2 * count + i: i for i in range(len(grads))},
        scratch_shapes=[
            pltpu.VMEM((total, span), BF16),
            pltpu.VMEM((total, span), BF16),
            pltpu.VMEM((span, 2 * hidden), BF16),
            pltpu.VMEM((hidden, span), BF16),
            pltpu.SemaphoreType.DMA((blocks, 2 * count)),
            pltpu.SemaphoreType.DMA((blocks, 3)),
        ],
        compiler_params=pltpu.CompilerParams(vmem_limit_bytes=16 * MIB),
        cost_estimate=pl.CostEstimate(
            flops=6 * total * span * hidden, bytes_accessed=4 * total * span + 6 * span * hidden, transcendentals=0
        ),
        name=name,
    )(*xe_parts, *diff_parts, *grads)


def swap(value, axis):
    return lax.ppermute(value, axis, [(0, 1), (1, 0)])


def far(value, axis, distance):
    return lax.ppermute(value, axis, [(i, i ^ distance) for i in range(lax.axis_size(axis))])


def together(*values):
    return lax.optimization_barrier(values)


def every_token_to_every_expert(
    layer_input, output_grad, routes, routing_weight, gate_proj, up_proj, down_proj
):
    tok_count, width = layer_input.shape
    top_count = routes.shape[1]
    lines = lax.axis_size("expert")
    expert = lax.axis_index("expert") * lax.axis_size("dp") + lax.axis_index("dp")
    expert_info = jnp.stack([expert, jnp.int32(top_count)]).astype(jnp.int32)
    packed = pack(layer_input, output_grad, routes, routing_weight)
    columns, across = {}, {}
    gate_w, up_w, packed = together(gate_proj, up_proj, packed)
    columns[1] = far(packed, "expert", 1)
    columns[2] = far(packed, "expert", 2)
    across[0] = swap(packed, "dp")
    wide_w = stage(gate_w, up_w)
    columns[0], columns[1], columns[2], across[0], wide_w = together(packed, columns[1], columns[2], across[0], wide_w)
    columns[3] = far(columns[0], "expert", 3)
    across[2] = swap(columns[2], "dp")
    across[1] = swap(columns[1], "dp")
    columns[3], across[1], across[2] = together(columns[3], across[1], across[2])
    across[3] = swap(columns[3], "dp")
    weights = (wide_w, down_proj)

    chunk = (2, 1, 0)
    shards = [columns[k] for k in chunk] + [across[k] for k in chunk]
    shards += [swap(shard, "sub") for shard in shards]
    keep, send, xe_0, diff_0 = expert_rows_chunk("rows_0", shards, expert_info, weights)
    diff_0, columns[3], across[3] = together(diff_0, columns[3], across[3])
    send, across[3] = together(send, across[3])
    paired = keep + swap(send, "sub").astype(F32)
    size = len(chunk) * tok_count
    own_0 = paired[2 * tok_count : size]
    away_0 = paired[size + 2 * tok_count :].astype(BF16)
    home_21 = paired[: 2 * tok_count] + swap(paired[size : size + 2 * tok_count].astype(BF16), "dp").astype(F32)

    shards = [columns[3], across[3]]
    shards += [swap(shard, "sub") for shard in shards]
    keep, send, xe_3, diff_3 = expert_rows_chunk("rows_3", shards, expert_info, weights)
    send, home_21 = together(send, home_21)
    back_2 = far(home_21[:tok_count].astype(BF16), "expert", 2)
    paired = keep + swap(send, "sub").astype(F32)
    home_3 = paired[:tok_count] + swap(paired[tok_count:].astype(BF16), "dp").astype(F32)
    home_3, away_0 = together(home_3, away_0)
    own_sum = own_0 + swap(away_0, "dp").astype(F32)
    back_3 = far(home_3.astype(BF16), "expert", 3)
    back_1 = far(home_21[tok_count:].astype(BF16), "expert", 1)
    gate_grads, up_grads, down_grads = weight_grads("grads", 0, width, (xe_0, xe_3), (diff_0, diff_3), ())
    gate_grads, back_1, back_2, back_3 = together(gate_grads, back_1, back_2, back_3)
    arrived = (back_1, back_2, back_3)
    total = own_sum
    for block in arrived:
        total = total + block.astype(F32)
    input_grad = total[:, :width].astype(BF16)
    products = total[:, width : width + top_count] + total[:, width + top_count : width + 2 * top_count]
    chosen = routes[:, :, None] == jnp.arange(top_count, dtype=jnp.int32)[None, None, :]
    routing_grad = jnp.sum(jnp.where(chosen, products[:, None, :], 0.0), axis=2)
    return (input_grad, routing_grad, gate_grads, up_grads, down_grads)


def expert_rows(inputs, gate_w, up_w, down_w):
    rows_x, rows_e = inputs
    leading = rows_x.shape[:-1]
    model_width = rows_x.shape[-1]
    hidden = gate_w.shape[1]
    flat_x = rows_x.reshape(-1, model_width)
    flat_e = rows_e.reshape(-1, model_width)
    contract = (((1,), (1,)), ((), ()))
    pre_gate = jnp.dot(flat_x, gate_w, preferred_element_type=jnp.float32)
    pre_up = jnp.dot(flat_x, up_w, preferred_element_type=jnp.float32)
    sigmoid_gate = jax.nn.sigmoid(pre_gate)
    silu_gate = pre_gate * sigmoid_gate
    hidden_act = silu_gate * pre_up
    hidden_low = hidden_act.astype(jnp.bfloat16)
    back_hidden = lax.dot_general(flat_e, down_w, contract, preferred_element_type=jnp.float32)
    product = jnp.sum(hidden_act * back_hidden, axis=1)
    silu_slope = sigmoid_gate * (1.0 + pre_gate * (1.0 - sigmoid_gate))
    diff_gate = (back_hidden * pre_up * silu_slope).astype(jnp.bfloat16)
    diff_up = (back_hidden * silu_gate).astype(jnp.bfloat16)
    row_grad = lax.dot_general(
        diff_gate, gate_w, contract, preferred_element_type=jnp.float32
    ) + lax.dot_general(diff_up, up_w, contract, preferred_element_type=jnp.float32)
    return (
        row_grad.reshape(leading + (model_width,)),
        product.reshape(leading),
        rows_x,
        rows_e,
        hidden_low.reshape(leading + (hidden,)),
        diff_gate.reshape(leading + (hidden,)),
        diff_up.reshape(leading + (hidden,)),
    )


def chosen_experts(layer_input, output_grad, routes, routing_weight, gate_proj, up_proj, down_proj):
    tok_count, model_width = layer_input.shape
    top_count = routes.shape[1]
    positions = lax.axis_size(("expert", "dp"))
    capacity = min(tok_count, 2 * tok_count * top_count // positions)
    row_count = tok_count * top_count
    slot_count = positions * capacity
    target = routes.reshape(-1)
    member = (target[:, None] == jnp.arange(positions, dtype=jnp.int32)[None, :]).astype(jnp.int32)
    earlier = jnp.cumsum(member, axis=0) - member
    slot_rank = jnp.sum(earlier * member, axis=1)
    slot_index = target * capacity + slot_rank
    source = (
        jnp.full((slot_count,), row_count, jnp.int32)
        .at[slot_index]
        .set(jnp.arange(row_count, dtype=jnp.int32))
    )
    filled = source < row_count
    picked = jnp.minimum(source, row_count - 1)
    token_index = picked // top_count
    row_scale = jnp.where(filled, routing_weight.reshape(-1)[picked], 0.0)
    send_x = jnp.where(
        filled[:, None], layer_input[token_index], jnp.zeros((), layer_input.dtype)
    ).reshape(positions, 1, capacity, model_width)
    send_e = (
        (row_scale[:, None] * output_grad[token_index].astype(jnp.float32))
        .astype(jnp.bfloat16)
        .reshape(positions, 1, capacity, model_width)
    )
    gate_w = gate_proj[0]
    up_w = up_proj[0]
    down_w = down_proj[0]
    hidden = gate_w.shape[1]
    paired = (
        lax.all_gather(send_x, "sub", axis=1, tiled=True),
        lax.all_gather(send_e, "sub", axis=1, tiled=True),
    )
    results = expert_rows(
        (
            lax.all_to_all(paired[0], ("expert", "dp"), split_axis=0, concat_axis=0, tiled=True),
            lax.all_to_all(paired[1], ("expert", "dp"), split_axis=0, concat_axis=0, tiled=True),
        ),
        gate_w,
        up_w,
        down_w,
    )
    row_part, product_part, rows_x, rows_e, hidden_low, diff_gate, diff_up = results
    returned = (
        lax.all_to_all(row_part, ("expert", "dp"), split_axis=0, concat_axis=0, tiled=True),
        lax.all_to_all(product_part, ("expert", "dp"), split_axis=0, concat_axis=0, tiled=True),
    )
    summed = (
        lax.psum_scatter(returned[0], "sub", scatter_dimension=1, tiled=True),
        lax.psum_scatter(returned[1], "sub", scatter_dimension=1, tiled=True),
    )
    back_rows = summed[0].astype(jnp.bfloat16)
    back_products = summed[1].astype(jnp.bfloat16)
    per_row = (
        back_rows.reshape(slot_count, model_width)[slot_index]
        .astype(jnp.float32)
        .reshape(tok_count, top_count, model_width)
    )
    input_grad = jnp.sum(per_row, axis=1).astype(jnp.bfloat16)
    routing_grad = (
        back_products.reshape(slot_count)[slot_index]
        .astype(jnp.float32)
        .reshape(tok_count, top_count)
        / routing_weight
    )
    over_rows = (((0,), (0,)), ((), ()))
    flat_x = rows_x.reshape(-1, model_width)
    flat_e = rows_e.reshape(-1, model_width)
    gate_grads = lax.dot_general(
        flat_x, diff_gate.reshape(-1, hidden), over_rows, preferred_element_type=jnp.float32
    ).astype(jnp.bfloat16)[None]
    up_grads = lax.dot_general(
        flat_x, diff_up.reshape(-1, hidden), over_rows, preferred_element_type=jnp.float32
    ).astype(jnp.bfloat16)[None]
    down_grads = lax.dot_general(
        hidden_low.reshape(-1, hidden), flat_e, over_rows, preferred_element_type=jnp.float32
    ).astype(jnp.bfloat16)[None]
    return (input_grad, routing_grad, gate_grads, up_grads, down_grads)


def per_device(layer_input, output_grad, routes, routing_weight, gate_proj, up_proj, down_proj):
    args = (layer_input, output_grad, routes, routing_weight, gate_proj, up_proj, down_proj)
    lines = lax.axis_size("expert")
    pairs = lax.axis_size("dp") == 2 and lax.axis_size("sub") == 2 and lines & (lines - 1) == 0
    if pairs and lines == 4 and 2 * lines == routes.shape[1] and gate_proj.shape[0] == 1:
        return every_token_to_every_expert(*args)
    return chosen_experts(*args)


def solution(mesh):
    placed = (
        P(("group", "expert", "dp", "sub"), None),
        P(("group", "expert", "dp", "sub"), None),
        P(("group", "expert", "dp", "sub"), None),
        P(("group", "expert", "dp", "sub"), None),
        P(("expert", "dp"), None, "sub"),
        P(("expert", "dp"), None, "sub"),
        P(("expert", "dp"), "sub", None),
    )
    return jax.shard_map(
        per_device,
        mesh=mesh,
        in_specs=placed,
        out_specs=(
            P(("group", "expert", "dp", "sub"), None),
            P(("group", "expert", "dp", "sub"), None),
            P(("group", "expert", "dp"), None, "sub"),
            P(("group", "expert", "dp"), None, "sub"),
            P(("group", "expert", "dp"), "sub", None),
        ),
        check_vma=False,
    )
```

```python
import functools

import jax
import jax.numpy as jnp
from jax import lax
from jax.experimental import pallas as pl
from jax.experimental.pallas import tpu as pltpu
from jax.sharding import PartitionSpec as P

F32 = jnp.float32
BF16 = jnp.bfloat16
SIDE = 128
NT = (((1,), (1,)), ((), ()))
TN = (((0,), (0,)), ((), ()))
MIB = 1024 * 1024


def split_columns(values, count, lane):
    high = values.astype(BF16)
    low = (values - high.astype(F32)).astype(BF16)
    zero = jnp.zeros_like(high)
    return jnp.where(lane < count, high, jnp.where(lane < 2 * count, low, zero))


def in_vmem(count):
    return [pl.BlockSpec(memory_space=pltpu.VMEM)] * count


def in_hbm(count):
    return [pl.BlockSpec(memory_space=pl.ANY)] * count


def held(*arrays):
    return [pltpu.with_memory_space_constraint(array, pltpu.VMEM) for array in arrays]


def left(*arrays):
    return [pltpu.with_memory_space_constraint(array, pltpu.HBM) for array in arrays]


def pack_kernel(x_ref, e_ref, routes_ref, weight_ref, out_ref, routes_held, weight_held, sems):
    tok_count, width = x_ref.shape
    top_count = routes_ref.shape[0]
    copies = [
        pltpu.make_async_copy(routes_ref, routes_held, sems.at[0]),
        pltpu.make_async_copy(weight_ref, weight_held, sems.at[1]),
        pltpu.make_async_copy(x_ref, out_ref.at[pl.ds(0, tok_count), pl.ds(0, width)], sems.at[2]),
        pltpu.make_async_copy(e_ref, out_ref.at[pl.ds(tok_count, tok_count), pl.ds(0, width)], sems.at[3]),
    ]
    for copy in copies:
        copy.start()
    out_ref[tok_count:, width:] = jnp.zeros((tok_count, SIDE), BF16)
    lane = lax.broadcasted_iota(jnp.int32, (tok_count, SIDE), 1)
    expert = lax.rem(lax.broadcasted_iota(jnp.int32, (SIDE, tok_count), 0), top_count)
    copies[0].wait()
    copies[1].wait()
    routes = routes_held[...]
    weight = weight_held[...]
    table = jnp.zeros((SIDE, tok_count), F32)
    for k in range(top_count):
        table += jnp.where(routes[k : k + 1, :] == expert, weight[k : k + 1, :], 0.0)
    out_ref[:tok_count, width:] = split_columns(table.T, top_count, lane)
    copies[2].wait()
    copies[3].wait()


def pack(x, e, routes, weight):
    tok_count, width = x.shape
    top_count = routes.shape[1]
    return pl.pallas_call(
        pack_kernel,
        in_specs=in_hbm(4),
        out_specs=in_vmem(1)[0],
        out_shape=pltpu.VMEM((2 * tok_count, width + SIDE), BF16),
        scratch_shapes=[
            pltpu.VMEM((top_count, tok_count), jnp.int32),
            pltpu.VMEM((top_count, tok_count), F32),
            pltpu.SemaphoreType.DMA((4,)),
        ],
        compiler_params=pltpu.CompilerParams(vmem_limit_bytes=4 * MIB),
        name="pack_tokens",
    )(*left(x, e, routes.T, weight.T))


def stage_kernel(gate_ref, up_ref, wide_ref, sems):
    _, width, hidden = gate_ref.shape
    pieces = sems.shape[1]
    block = width // pieces
    copies = []
    for i in range(pieces):
        here = pl.ds(i * block, block)
        copies += [
            pltpu.make_async_copy(gate_ref.at[0, here], wide_ref.at[here, pl.ds(0, hidden)], sems.at[0, i]),
            pltpu.make_async_copy(up_ref.at[0, here], wide_ref.at[here, pl.ds(hidden, hidden)], sems.at[1, i]),
        ]
    for copy in copies:
        copy.start()
    for copy in copies:
        copy.wait()


def stage(gate_w, up_w):
    _, width, hidden = gate_w.shape
    return pl.pallas_call(
        stage_kernel,
        in_specs=in_hbm(2),
        out_specs=in_vmem(1)[0],
        out_shape=pltpu.VMEM((width, 2 * hidden), BF16),
        scratch_shapes=[pltpu.SemaphoreType.DMA((2, 4))],
        compiler_params=pltpu.CompilerParams(vmem_limit_bytes=8 * MIB),
        cost_estimate=pl.CostEstimate(flops=1, bytes_accessed=1, transcendentals=0),
        name="stage_weights",
    )(*left(gate_w, up_w))


def rows_kernel(shards, experts, expert_ref, *refs):
    shard_refs = refs[:shards]
    wide_ref, down_ref, keep_ref, send_ref, xe_ref, diff_ref, tall_ref, table_ref, sems = refs[shards:]
    tok_count = shard_refs[0].shape[0] // 2
    rows = shards * tok_count
    half = rows // 2
    hidden, width = tall_ref.shape
    pieces = 4
    block = hidden // pieces
    down_copies = [
        (down_ref.at[0, pl.ds(i * block, block)], tall_ref.at[pl.ds(i * block, block)]) for i in range(pieces)
    ]
    x_copies, e_copies = [], []
    for i, ref in enumerate(shard_refs):
        here = pl.ds(i * tok_count, tok_count)
        x_copies.append((ref.at[pl.ds(0, tok_count), pl.ds(0, width)], xe_ref.at[here]))
        e_copies.append(
            (ref.at[pl.ds(tok_count, tok_count), pl.ds(0, width)], xe_ref.at[pl.ds(rows + i * tok_count, tok_count)])
        )
        e_copies.append((ref.at[pl.ds(0, tok_count), pl.ds(width, SIDE)], table_ref.at[here]))
    copies = [
        pltpu.make_async_copy(src, dst, sems.at[i]) for i, (src, dst) in enumerate(x_copies + down_copies + e_copies)
    ]
    for copy in copies:
        copy.start()
    chosen = expert_ref[:1, :] != 0
    for copy in copies[:shards]:
        copy.wait()
    pre = jnp.dot(xe_ref[:rows, :], wide_ref[...], preferred_element_type=F32)
    for copy in copies[shards:]:
        copy.wait()
    weight = jnp.sum(jnp.where(chosen, table_ref[...].astype(F32), 0.0), axis=1, keepdims=True)
    back = lax.dot_general(xe_ref[rows:, :], tall_ref[...], NT, preferred_element_type=F32)
    pre_gate, pre_up = pre[:, :hidden], pre[:, hidden:]
    sig = jax.nn.sigmoid(pre_gate)
    silu = pre_gate * sig
    act = silu * pre_up
    product = jnp.sum(act * back, axis=1, keepdims=True)
    back = back * weight
    diff_gate = (back * pre_up * (sig * (1.0 + pre_gate * (1.0 - sig)))).astype(BF16)
    diff_up = (back * silu).astype(BF16)
    diff = jnp.concatenate([diff_gate, diff_up], axis=1)
    diff_ref[:, : 2 * hidden] = diff
    diff_ref[:, 2 * hidden :] = (act * weight).astype(BF16)
    block = 512
    for c in range(0, width, block):
        part = lax.dot_general(diff, wide_ref[c : c + block, :], NT, preferred_element_type=F32)
        keep_ref[:, c : c + block] = part[:half]
        send_ref[:, c : c + block] = part[half:].astype(BF16)
    lane = lax.broadcasted_iota(jnp.int32, (rows, SIDE), 1)
    side = split_columns(jnp.where(chosen, product, 0.0), experts, lane)
    keep_ref[:, width:] = side[:half].astype(F32)
    send_ref[:, width:] = side[half:]


def expert_rows_chunk(name, shards, experts, expert_info, weights):
    count = len(shards)
    tok_count = shards[0].shape[0] // 2
    wide = shards[0].shape[1]
    width = wide - SIDE
    rows = count * tok_count
    hidden = weights[1].shape[1]
    return pl.pallas_call(
        functools.partial(rows_kernel, count, experts),
        in_specs=in_vmem(1) + in_hbm(count) + in_vmem(1) + in_hbm(1),
        out_specs=in_vmem(4),
        out_shape=[
            pltpu.VMEM((rows // 2, wide), F32),
            pltpu.VMEM((rows // 2, wide), BF16),
            pltpu.VMEM((2 * rows, width), BF16),
            pltpu.VMEM((rows, 3 * hidden), BF16),
        ],
        scratch_shapes=[
            pltpu.VMEM((hidden, width), BF16),
            pltpu.VMEM((rows, SIDE), BF16),
            pltpu.SemaphoreType.DMA((3 * count + 4,)),
        ],
        compiler_params=pltpu.CompilerParams(vmem_limit_bytes=16 * MIB),
        cost_estimate=pl.CostEstimate(flops=1, bytes_accessed=1, transcendentals=0),
        name=name,
    )(expert_info, *(left(*shards) if count > 4 else shards), weights[0], *left(weights[1]))


def grads_kernel(parts, *refs):
    xe_refs = refs[:parts]
    diff_refs = refs[parts : 2 * parts]
    gate_out, up_out, down_out, both_ref, down_ref, out_sems = refs[2 * parts :]
    hidden = gate_out.shape[2]
    width = gate_out.shape[1]
    block = width // out_sems.shape[0]
    diffs = jnp.concatenate([ref[:, : 2 * hidden] for ref in diff_refs], axis=0)
    hidden_t = jnp.concatenate([ref[:, 2 * hidden :] for ref in diff_refs], axis=0).T
    leaving = []
    for i, c in enumerate(range(0, width, block)):
        columns = slice(c, c + block)
        here = pl.ds(c, block)
        x = jnp.concatenate([ref[: ref.shape[0] // 2, columns] for ref in xe_refs], axis=0)
        e = jnp.concatenate([ref[ref.shape[0] // 2 :, columns] for ref in xe_refs], axis=0)
        both_ref[columns, :] = lax.dot_general(x, diffs, TN, preferred_element_type=F32).astype(BF16)
        down_ref[:, columns] = jnp.dot(hidden_t, e, preferred_element_type=F32).astype(BF16)
        copies = [
            pltpu.make_async_copy(both_ref.at[here, pl.ds(0, hidden)], gate_out.at[0, here], out_sems.at[i, 0]),
            pltpu.make_async_copy(both_ref.at[here, pl.ds(hidden, hidden)], up_out.at[0, here], out_sems.at[i, 1]),
            pltpu.make_async_copy(down_ref.at[:, here], down_out.at[0, :, here], out_sems.at[i, 2]),
        ]
        for copy in copies:
            copy.start()
        leaving += copies
    for copy in leaving:
        copy.wait()


def weight_grads(xe_parts, diff_parts):
    count = len(xe_parts)
    width = xe_parts[0].shape[1]
    hidden = diff_parts[0].shape[1] // 3
    total = sum(part.shape[0] for part in diff_parts)
    return pl.pallas_call(
        functools.partial(grads_kernel, count),
        in_specs=in_vmem(2 * count),
        out_specs=in_hbm(3),
        out_shape=[
            jax.ShapeDtypeStruct((1, width, hidden), BF16),
            jax.ShapeDtypeStruct((1, width, hidden), BF16),
            jax.ShapeDtypeStruct((1, hidden, width), BF16),
        ],
        scratch_shapes=[
            pltpu.VMEM((width, 2 * hidden), BF16),
            pltpu.VMEM((hidden, width), BF16),
            pltpu.SemaphoreType.DMA((2, 3)),
        ],
        compiler_params=pltpu.CompilerParams(vmem_limit_bytes=24 * MIB),
        cost_estimate=pl.CostEstimate(
            flops=6 * total * width * hidden, bytes_accessed=4 * total * width + 6 * width * hidden, transcendentals=0
        ),
        name="weight_grads",
    )(*xe_parts, *diff_parts)


def finish_kernel(parts, own_ref, *refs):
    routes_ref, input_ref, routing_ref = refs[parts:]
    width = input_ref.shape[1]
    top_count = routes_ref.shape[0]
    total = own_ref[...]
    for ref in refs[:parts]:
        total = total + ref[...].astype(F32)
    input_ref[...] = total[:, :width].astype(BF16)
    side = total[:, width:].T
    products = side[:top_count] + side[top_count : 2 * top_count]
    routes = routes_ref[...]
    picked = jnp.zeros(routes.shape, F32)
    for e in range(top_count):
        picked += jnp.where(routes == e, products[e : e + 1, :], 0.0)
    routing_ref[...] = picked


def finish(own_sum, arrived, routes):
    tok_count, top_count = routes.shape
    width = own_sum.shape[1] - SIDE
    input_grad, routing_grad = pl.pallas_call(
        functools.partial(finish_kernel, len(arrived)),
        in_specs=in_vmem(2 + len(arrived)),
        out_specs=in_vmem(2),
        out_shape=[
            jax.ShapeDtypeStruct((tok_count, width), BF16),
            jax.ShapeDtypeStruct((top_count, tok_count), F32),
        ],
        compiler_params=pltpu.CompilerParams(vmem_limit_bytes=4 * MIB),
        name="finish",
    )(own_sum, *arrived, routes.T)
    return input_grad, routing_grad.T


def swap(value, axis):
    return lax.ppermute(value, axis, [(0, 1), (1, 0)])


def far(value, axis, distance):
    return lax.ppermute(value, axis, [(i, i ^ distance) for i in range(lax.axis_size(axis))])


def together(*values):
    return lax.optimization_barrier(values)


def every_token_to_every_expert(
    layer_input, output_grad, routes, routing_weight, gate_proj, up_proj, down_proj
):
    tok_count, width = layer_input.shape
    top_count = routes.shape[1]
    lines = lax.axis_size("expert")
    expert = lax.axis_index("expert") * lax.axis_size("dp") + lax.axis_index("dp")
    lane = lax.broadcasted_iota(jnp.int32, (8, SIDE), 1)
    expert_info = ((lane == expert) | (lane == expert + top_count)).astype(jnp.int32)
    packed = pack(layer_input, output_grad, routes, routing_weight)
    columns, across = {}, {}
    gate_w, up_w, packed = together(gate_proj, up_proj, packed)
    columns[1] = far(packed, "expert", 1)
    columns[2] = far(packed, "expert", 2)
    across[0] = swap(packed, "dp")
    wide_w = stage(gate_w, up_w)
    columns[0], columns[1], columns[2], across[0], wide_w = together(packed, columns[1], columns[2], across[0], wide_w)
    columns[3] = far(columns[0], "expert", 3)
    across[2] = swap(columns[2], "dp")
    across[1] = swap(columns[1], "dp")
    columns[3], across[1], across[2] = together(columns[3], across[1], across[2])
    across[3] = swap(columns[3], "dp")
    weights = (wide_w, down_proj)

    shards = [columns[2], across[2], columns[1], columns[0], across[1], across[0]]
    shards += [swap(shard, "sub") for shard in shards]
    keep, send, xe_0, diff_0 = expert_rows_chunk("rows_0", shards, top_count, expert_info, weights)
    diff_0, columns[3], across[3] = together(diff_0, columns[3], across[3])
    send, across[3] = together(send, across[3])
    rows = tok_count
    paired_2 = keep[: 2 * rows] + swap(send[: 2 * rows], "sub").astype(F32)
    home_2 = paired_2[:rows] + swap(paired_2[rows:].astype(BF16), "dp").astype(F32)
    paired_10 = keep[2 * rows :] + swap(send[2 * rows :], "sub").astype(F32)
    away_1, away_0 = paired_10[2 * rows : 3 * rows].astype(BF16), paired_10[3 * rows :].astype(BF16)

    shards = [columns[3], across[3]]
    shards += [swap(shard, "sub") for shard in shards]
    keep, send, xe_3, diff_3 = expert_rows_chunk("rows_3", shards, top_count, expert_info, weights)
    send, home_2 = together(send, home_2)
    back_2 = far(home_2.astype(BF16), "expert", 2)
    paired_3 = keep + swap(send, "sub").astype(F32)
    home_3 = paired_3[:rows] + swap(paired_3[rows:].astype(BF16), "dp").astype(F32)
    home_1 = paired_10[:rows] + swap(away_1, "dp").astype(F32)
    home_3, away_0, back_2 = together(home_3, away_0, back_2)
    back_0 = swap(away_0, "dp")
    back_3 = far(home_3.astype(BF16), "expert", 3)
    back_1 = far(home_1.astype(BF16), "expert", 1)
    gate_grads, up_grads, down_grads = weight_grads((xe_0, xe_3), (diff_0, diff_3))
    gate_grads, back_1, back_2, back_3 = together(gate_grads, back_1, back_2, back_3)
    arrived = (back_0, back_1, back_2, back_3)
    input_grad, routing_grad = finish(paired_10[rows : 2 * rows], arrived, routes)
    return (input_grad, routing_grad, gate_grads, up_grads, down_grads)


def expert_rows(inputs, gate_w, up_w, down_w):
    rows_x, rows_e = inputs
    leading = rows_x.shape[:-1]
    model_width = rows_x.shape[-1]
    hidden = gate_w.shape[1]
    flat_x = rows_x.reshape(-1, model_width)
    flat_e = rows_e.reshape(-1, model_width)
    contract = (((1,), (1,)), ((), ()))
    pre_gate = jnp.dot(flat_x, gate_w, preferred_element_type=jnp.float32)
    pre_up = jnp.dot(flat_x, up_w, preferred_element_type=jnp.float32)
    sigmoid_gate = jax.nn.sigmoid(pre_gate)
    silu_gate = pre_gate * sigmoid_gate
    hidden_act = silu_gate * pre_up
    hidden_low = hidden_act.astype(jnp.bfloat16)
    back_hidden = lax.dot_general(flat_e, down_w, contract, preferred_element_type=jnp.float32)
    product = jnp.sum(hidden_act * back_hidden, axis=1)
    silu_slope = sigmoid_gate * (1.0 + pre_gate * (1.0 - sigmoid_gate))
    diff_gate = (back_hidden * pre_up * silu_slope).astype(jnp.bfloat16)
    diff_up = (back_hidden * silu_gate).astype(jnp.bfloat16)
    row_grad = lax.dot_general(
        diff_gate, gate_w, contract, preferred_element_type=jnp.float32
    ) + lax.dot_general(diff_up, up_w, contract, preferred_element_type=jnp.float32)
    return (
        row_grad.reshape(leading + (model_width,)),
        product.reshape(leading),
        rows_x,
        rows_e,
        hidden_low.reshape(leading + (hidden,)),
        diff_gate.reshape(leading + (hidden,)),
        diff_up.reshape(leading + (hidden,)),
    )


def chosen_experts(layer_input, output_grad, routes, routing_weight, gate_proj, up_proj, down_proj):
    tok_count, model_width = layer_input.shape
    top_count = routes.shape[1]
    positions = lax.axis_size(("expert", "dp"))
    capacity = min(tok_count, 2 * tok_count * top_count // positions)
    row_count = tok_count * top_count
    slot_count = positions * capacity
    target = routes.reshape(-1)
    member = (target[:, None] == jnp.arange(positions, dtype=jnp.int32)[None, :]).astype(jnp.int32)
    earlier = jnp.cumsum(member, axis=0) - member
    slot_rank = jnp.sum(earlier * member, axis=1)
    slot_index = target * capacity + slot_rank
    source = (
        jnp.full((slot_count,), row_count, jnp.int32)
        .at[slot_index]
        .set(jnp.arange(row_count, dtype=jnp.int32))
    )
    filled = source < row_count
    picked = jnp.minimum(source, row_count - 1)
    token_index = picked // top_count
    row_scale = jnp.where(filled, routing_weight.reshape(-1)[picked], 0.0)
    send_x = jnp.where(
        filled[:, None], layer_input[token_index], jnp.zeros((), layer_input.dtype)
    ).reshape(positions, 1, capacity, model_width)
    send_e = (
        (row_scale[:, None] * output_grad[token_index].astype(jnp.float32))
        .astype(jnp.bfloat16)
        .reshape(positions, 1, capacity, model_width)
    )
    gate_w = gate_proj[0]
    up_w = up_proj[0]
    down_w = down_proj[0]
    hidden = gate_w.shape[1]
    paired = (
        lax.all_gather(send_x, "sub", axis=1, tiled=True),
        lax.all_gather(send_e, "sub", axis=1, tiled=True),
    )
    results = expert_rows(
        (
            lax.all_to_all(paired[0], ("expert", "dp"), split_axis=0, concat_axis=0, tiled=True),
            lax.all_to_all(paired[1], ("expert", "dp"), split_axis=0, concat_axis=0, tiled=True),
        ),
        gate_w,
        up_w,
        down_w,
    )
    row_part, product_part, rows_x, rows_e, hidden_low, diff_gate, diff_up = results
    returned = (
        lax.all_to_all(row_part, ("expert", "dp"), split_axis=0, concat_axis=0, tiled=True),
        lax.all_to_all(product_part, ("expert", "dp"), split_axis=0, concat_axis=0, tiled=True),
    )
    summed = (
        lax.psum_scatter(returned[0], "sub", scatter_dimension=1, tiled=True),
        lax.psum_scatter(returned[1], "sub", scatter_dimension=1, tiled=True),
    )
    back_rows = summed[0].astype(jnp.bfloat16)
    back_products = summed[1].astype(jnp.bfloat16)
    per_row = (
        back_rows.reshape(slot_count, model_width)[slot_index]
        .astype(jnp.float32)
        .reshape(tok_count, top_count, model_width)
    )
    input_grad = jnp.sum(per_row, axis=1).astype(jnp.bfloat16)
    routing_grad = (
        back_products.reshape(slot_count)[slot_index]
        .astype(jnp.float32)
        .reshape(tok_count, top_count)
        / routing_weight
    )
    over_rows = (((0,), (0,)), ((), ()))
    flat_x = rows_x.reshape(-1, model_width)
    flat_e = rows_e.reshape(-1, model_width)
    gate_grads = lax.dot_general(
        flat_x, diff_gate.reshape(-1, hidden), over_rows, preferred_element_type=jnp.float32
    ).astype(jnp.bfloat16)[None]
    up_grads = lax.dot_general(
        flat_x, diff_up.reshape(-1, hidden), over_rows, preferred_element_type=jnp.float32
    ).astype(jnp.bfloat16)[None]
    down_grads = lax.dot_general(
        hidden_low.reshape(-1, hidden), flat_e, over_rows, preferred_element_type=jnp.float32
    ).astype(jnp.bfloat16)[None]
    return (input_grad, routing_grad, gate_grads, up_grads, down_grads)


def per_device(layer_input, output_grad, routes, routing_weight, gate_proj, up_proj, down_proj):
    args = (layer_input, output_grad, routes, routing_weight, gate_proj, up_proj, down_proj)
    lines = lax.axis_size("expert")
    pairs = lax.axis_size("dp") == 2 and lax.axis_size("sub") == 2 and lines & (lines - 1) == 0
    if pairs and lines == 4 and 2 * lines == routes.shape[1] and gate_proj.shape[0] == 1:
        return every_token_to_every_expert(*args)
    return chosen_experts(*args)


def solution(mesh):
    placed = (
        P(("group", "expert", "dp", "sub"), None),
        P(("group", "expert", "dp", "sub"), None),
        P(("group", "expert", "dp", "sub"), None),
        P(("group", "expert", "dp", "sub"), None),
        P(("expert", "dp"), None, "sub"),
        P(("expert", "dp"), None, "sub"),
        P(("expert", "dp"), "sub", None),
    )
    return jax.shard_map(
        per_device,
        mesh=mesh,
        in_specs=placed,
        out_specs=(
            P(("group", "expert", "dp", "sub"), None),
            P(("group", "expert", "dp", "sub"), None),
            P(("group", "expert", "dp"), None, "sub"),
            P(("group", "expert", "dp"), None, "sub"),
            P(("group", "expert", "dp"), "sub", None),
        ),
        check_vma=False,
    )
```

```python
import functools

import jax
import jax.numpy as jnp
from jax import lax
from jax.experimental import pallas as pl
from jax.experimental.pallas import tpu as pltpu
from jax.sharding import PartitionSpec as P

F32 = jnp.float32
BF16 = jnp.bfloat16
SIDE = 128
FOLD = 16
NT = (((1,), (1,)), ((), ()))
TN = (((0,), (0,)), ((), ()))
MIB = 1024 * 1024


def split_columns(values, count, lane):
    high = values.astype(BF16)
    low = (values - high.astype(F32)).astype(BF16)
    zero = jnp.zeros_like(high)
    return jnp.where(lane < count, high, jnp.where(lane < 2 * count, low, zero))


def in_vmem(count):
    return [pl.BlockSpec(memory_space=pltpu.VMEM)] * count


def in_hbm(count):
    return [pl.BlockSpec(memory_space=pl.ANY)] * count


def held(*arrays):
    return [pltpu.with_memory_space_constraint(array, pltpu.VMEM) for array in arrays]


def left(*arrays):
    return [pltpu.with_memory_space_constraint(array, pltpu.HBM) for array in arrays]


def pack_kernel(x_ref, e_ref, routes_ref, weight_ref, out_ref, routes_held, weight_held, sems):
    tok_count, width = x_ref.shape
    top_count = routes_ref.shape[0]
    folds = tok_count // FOLD
    copies = [
        pltpu.make_async_copy(routes_ref, routes_held, sems.at[0]),
        pltpu.make_async_copy(weight_ref, weight_held, sems.at[1]),
    ]
    for i in range(2 * folds):
        source = (x_ref, e_ref)[i // folds].at[pl.ds(i % folds * FOLD, FOLD)]
        copies.append(pltpu.make_async_copy(source, out_ref.at[:, pl.ds(i * width, width)], sems.at[2 + i]))
    for copy in copies:
        copy.start()
    lane = lax.broadcasted_iota(jnp.int32, (FOLD, SIDE), 1)
    expert = lax.rem(lax.broadcasted_iota(jnp.int32, (SIDE, tok_count), 0), top_count)
    copies[0].wait()
    copies[1].wait()
    routes = routes_held[...]
    weight = weight_held[...]
    table = jnp.zeros((SIDE, tok_count), F32)
    for k in range(top_count):
        table += jnp.where(routes[k : k + 1, :] == expert, weight[k : k + 1, :], 0.0)
    table = table.T
    side = jnp.zeros((FOLD, SIDE), BF16)
    for i in range(folds):
        here = split_columns(table[i * FOLD : (i + 1) * FOLD], top_count, lane - 2 * i * top_count)
        side = jnp.where(lane < 2 * i * top_count, side, here)
    out_ref[:, 2 * folds * width :] = side
    for copy in copies[2:]:
        copy.wait()


def pack(x, e, routes, weight):
    tok_count, width = x.shape
    top_count = routes.shape[1]
    blocks = 2 * tok_count // FOLD
    return pl.pallas_call(
        pack_kernel,
        in_specs=in_hbm(4),
        out_specs=in_vmem(1)[0],
        out_shape=pltpu.VMEM((FOLD, blocks * width + SIDE), BF16),
        scratch_shapes=[
            pltpu.VMEM((top_count, tok_count), jnp.int32),
            pltpu.VMEM((top_count, tok_count), F32),
            pltpu.SemaphoreType.DMA((2 + blocks,)),
        ],
        compiler_params=pltpu.CompilerParams(vmem_limit_bytes=4 * MIB),
        name="pack_tokens",
    )(*left(x, e, routes.T, weight.T))


def stage_kernel(gate_ref, up_ref, wide_ref, sems):
    _, width, hidden = gate_ref.shape
    pieces = sems.shape[1]
    block = width // pieces
    copies = []
    for i in range(pieces):
        here = pl.ds(i * block, block)
        copies += [
            pltpu.make_async_copy(gate_ref.at[0, here], wide_ref.at[here, pl.ds(0, hidden)], sems.at[0, i]),
            pltpu.make_async_copy(up_ref.at[0, here], wide_ref.at[here, pl.ds(hidden, hidden)], sems.at[1, i]),
        ]
    for copy in copies:
        copy.start()
    for copy in copies:
        copy.wait()


def stage(gate_w, up_w):
    _, width, hidden = gate_w.shape
    return pl.pallas_call(
        stage_kernel,
        in_specs=in_hbm(2),
        out_specs=in_vmem(1)[0],
        out_shape=pltpu.VMEM((width, 2 * hidden), BF16),
        scratch_shapes=[pltpu.SemaphoreType.DMA((2, 4))],
        compiler_params=pltpu.CompilerParams(vmem_limit_bytes=8 * MIB),
        cost_estimate=pl.CostEstimate(flops=1, bytes_accessed=1, transcendentals=0),
        name="stage_weights",
    )(*left(gate_w, up_w))


def rows_kernel(shards, experts, first, expert_ref, *refs):
    shard_refs = refs[:shards]
    wide_ref, down_ref, keep_ref, send_ref, xe_ref, diff_ref = refs[shards : shards + 6]
    width = xe_ref.shape[1]
    rows = xe_ref.shape[0] // 2
    tok_count = rows // shards
    folds = tok_count // FOLD
    half = rows // 2
    hidden = diff_ref.shape[1] // 3
    chosen = expert_ref[:1, :] != 0
    lane = lax.broadcasted_iota(jnp.int32, (1, SIDE), 1)
    if first:
        tall_ref, table_ref, sems = refs[shards + 6 :]
        pieces = 4
        block = hidden // pieces
        copies = []
        for i, ref in enumerate(shard_refs):
            for j in range(folds):
                here = pl.ds(i * tok_count + j * FOLD, FOLD)
                copies.append((ref.at[:, pl.ds(j * width, width)], xe_ref.at[here]))
        count = len(copies)
        for i in range(pieces):
            here = pl.ds(i * block, block)
            copies.append((down_ref.at[0, here], tall_ref.at[here]))
        for i, ref in enumerate(shard_refs):
            for j in range(folds):
                here = pl.ds(rows + i * tok_count + j * FOLD, FOLD)
                copies.append((ref.at[:, pl.ds((folds + j) * width, width)], xe_ref.at[here]))
            copies.append((ref.at[:, pl.ds(2 * folds * width, SIDE)], table_ref.at[pl.ds(i * FOLD, FOLD)]))
        copies = [pltpu.make_async_copy(src, dst, sems.at[i]) for i, (src, dst) in enumerate(copies)]
        for copy in copies:
            copy.start()
        for copy in copies[:count]:
            copy.wait()
        pre = jnp.dot(xe_ref[:rows, :], wide_ref[...], preferred_element_type=F32)
        for copy in copies[count:]:
            copy.wait()
        e = xe_ref[rows:, :]
        table = table_ref[...].astype(F32)
    else:
        tall_ref = down_ref

        def pick(start):
            return jnp.concatenate(
                [ref[:, (start + j) * width : (start + j + 1) * width] for ref in shard_refs for j in range(folds)], axis=0
            )

        x, e = pick(0), pick(folds)
        xe_ref[:rows, :] = x
        xe_ref[rows:, :] = e
        pre = jnp.dot(x, wide_ref[...], preferred_element_type=F32)
        table = jnp.concatenate([ref[:, 2 * folds * width :] for ref in shard_refs], axis=0).astype(F32)
    weights = []
    for j in range(folds):
        mine = chosen & (lane >= 2 * j * experts) & (lane < 2 * (j + 1) * experts)
        weights.append(jnp.sum(jnp.where(mine, table, 0.0), axis=1, keepdims=True))
    weight = jnp.concatenate(
        [weights[j][i * FOLD : (i + 1) * FOLD] for i in range(shards) for j in range(folds)], axis=0
    )
    back = lax.dot_general(e, tall_ref[...], NT, preferred_element_type=F32)
    pre_gate, pre_up = pre[:, :hidden], pre[:, hidden:]
    sig = jax.nn.sigmoid(pre_gate)
    silu = pre_gate * sig
    act = silu * pre_up
    product = jnp.sum(act * back, axis=1, keepdims=True)
    back = back * weight
    diff_gate = (back * pre_up * (sig * (1.0 + pre_gate * (1.0 - sig)))).astype(BF16)
    diff_up = (back * silu).astype(BF16)
    diff = jnp.concatenate([diff_gate, diff_up], axis=1)
    diff_ref[:, : 2 * hidden] = diff
    diff_ref[:, 2 * hidden :] = (act * weight).astype(BF16)
    block = 512
    for c in range(0, width, block):
        part = lax.dot_general(diff, wide_ref[c : c + block, :], NT, preferred_element_type=F32)
        keep_ref[:, c : c + block] = part[:half]
        send_ref[:, c : c + block] = part[half:].astype(BF16)
    lane = lax.broadcasted_iota(jnp.int32, (rows, SIDE), 1)
    side = split_columns(jnp.where(chosen, product, 0.0), experts, lane)
    keep_ref[:, width:] = side[:half].astype(F32)
    send_ref[:, width:] = side[half:]


def expert_rows_chunk(name, shards, tok_count, experts, expert_info, weights):
    count = len(shards)
    first = weights[1].ndim == 3
    width = (shards[0].shape[1] - SIDE) * FOLD // (2 * tok_count)
    rows = count * tok_count
    hidden = weights[0].shape[1] // 2
    out_shape = [
        pltpu.VMEM((rows // 2, width + SIDE), F32),
        pltpu.VMEM((rows // 2, width + SIDE), BF16),
        pltpu.VMEM((2 * rows, width), BF16),
        pltpu.VMEM((rows, 3 * hidden), BF16),
    ]
    scratch_shapes = []
    if first:
        out_shape.append(pltpu.VMEM((hidden, width), BF16))
        scratch_shapes = [
            pltpu.VMEM((count * FOLD, SIDE), BF16),
            pltpu.SemaphoreType.DMA((count * (2 * tok_count // FOLD + 1) + 4,)),
        ]
    return pl.pallas_call(
        functools.partial(rows_kernel, count, experts, first),
        in_specs=in_vmem(1) + (in_hbm(count) + in_vmem(1) + in_hbm(1) if first else in_vmem(count + 2)),
        out_specs=in_vmem(len(out_shape)),
        out_shape=out_shape,
        scratch_shapes=scratch_shapes,
        compiler_params=pltpu.CompilerParams(vmem_limit_bytes=16 * MIB),
        cost_estimate=pl.CostEstimate(flops=1, bytes_accessed=1, transcendentals=0),
        name=name,
    )(expert_info, *(left(*shards) if first else shards), weights[0], *(left(weights[1]) if first else (weights[1],)))


def grads_kernel(parts, *refs):
    xe_refs = refs[:parts]
    diff_refs = refs[parts : 2 * parts]
    gate_out, up_out, down_out, both_ref, down_ref, out_sems = refs[2 * parts :]
    hidden = gate_out.shape[2]
    width = gate_out.shape[1]
    block = width // out_sems.shape[0]
    diffs = jnp.concatenate([ref[:, : 2 * hidden] for ref in diff_refs], axis=0)
    hidden_t = jnp.concatenate([ref[:, 2 * hidden :] for ref in diff_refs], axis=0).T
    leaving = []
    for i, c in enumerate(range(0, width, block)):
        columns = slice(c, c + block)
        here = pl.ds(c, block)
        x = jnp.concatenate([ref[: ref.shape[0] // 2, columns] for ref in xe_refs], axis=0)
        e = jnp.concatenate([ref[ref.shape[0] // 2 :, columns] for ref in xe_refs], axis=0)
        both_ref[columns, :] = lax.dot_general(x, diffs, TN, preferred_element_type=F32).astype(BF16)
        down_ref[:, columns] = jnp.dot(hidden_t, e, preferred_element_type=F32).astype(BF16)
        copies = [
            pltpu.make_async_copy(both_ref.at[here, pl.ds(0, hidden)], gate_out.at[0, here], out_sems.at[i, 0]),
            pltpu.make_async_copy(both_ref.at[here, pl.ds(hidden, hidden)], up_out.at[0, here], out_sems.at[i, 1]),
            pltpu.make_async_copy(down_ref.at[:, here], down_out.at[0, :, here], out_sems.at[i, 2]),
        ]
        for copy in copies:
            copy.start()
        leaving += copies
    for copy in leaving:
        copy.wait()


def weight_grads(xe_parts, diff_parts):
    count = len(xe_parts)
    width = xe_parts[0].shape[1]
    hidden = diff_parts[0].shape[1] // 3
    total = sum(part.shape[0] for part in diff_parts)
    return pl.pallas_call(
        functools.partial(grads_kernel, count),
        in_specs=in_vmem(2 * count),
        out_specs=in_hbm(3),
        out_shape=[
            jax.ShapeDtypeStruct((1, width, hidden), BF16),
            jax.ShapeDtypeStruct((1, width, hidden), BF16),
            jax.ShapeDtypeStruct((1, hidden, width), BF16),
        ],
        scratch_shapes=[
            pltpu.VMEM((width, 2 * hidden), BF16),
            pltpu.VMEM((hidden, width), BF16),
            pltpu.SemaphoreType.DMA((2, 3)),
        ],
        compiler_params=pltpu.CompilerParams(vmem_limit_bytes=24 * MIB),
        cost_estimate=pl.CostEstimate(
            flops=6 * total * width * hidden, bytes_accessed=4 * total * width + 6 * width * hidden, transcendentals=0
        ),
        name="weight_grads",
    )(*xe_parts, *diff_parts)


def finish_kernel(parts, own_ref, *refs):
    routes_ref, input_ref, routing_ref = refs[parts:]
    width = input_ref.shape[1]
    top_count = routes_ref.shape[0]
    total = own_ref[...]
    for ref in refs[:parts]:
        total = total + ref[...].astype(F32)
    input_ref[...] = total[:, :width].astype(BF16)
    side = total[:, width:].T
    products = side[:top_count] + side[top_count : 2 * top_count]
    routes = routes_ref[...]
    picked = jnp.zeros(routes.shape, F32)
    for e in range(top_count):
        picked += jnp.where(routes == e, products[e : e + 1, :], 0.0)
    routing_ref[...] = picked


def finish(own_sum, arrived, routes):
    tok_count, top_count = routes.shape
    width = own_sum.shape[1] - SIDE
    input_grad, routing_grad = pl.pallas_call(
        functools.partial(finish_kernel, len(arrived)),
        in_specs=in_vmem(2 + len(arrived)),
        out_specs=in_vmem(2),
        out_shape=[
            jax.ShapeDtypeStruct((tok_count, width), BF16),
            jax.ShapeDtypeStruct((top_count, tok_count), F32),
        ],
        compiler_params=pltpu.CompilerParams(vmem_limit_bytes=4 * MIB),
        name="finish",
    )(own_sum, *arrived, routes.T)
    return input_grad, routing_grad.T


def swap(value, axis):
    return lax.ppermute(value, axis, [(0, 1), (1, 0)])


def far(value, axis, distance):
    return lax.ppermute(value, axis, [(i, i ^ distance) for i in range(lax.axis_size(axis))])


def together(*values):
    return lax.optimization_barrier(values)


def every_token_to_every_expert(
    layer_input, output_grad, routes, routing_weight, gate_proj, up_proj, down_proj
):
    tok_count, width = layer_input.shape
    top_count = routes.shape[1]
    lines = lax.axis_size("expert")
    expert = lax.axis_index("expert") * lax.axis_size("dp") + lax.axis_index("dp")
    lane = lax.broadcasted_iota(jnp.int32, (8, SIDE), 1)
    expert_info = (lax.rem(lane, top_count) == expert).astype(jnp.int32)
    packed = pack(layer_input, output_grad, routes, routing_weight)
    columns, across = {}, {}
    gate_w, up_w, packed = together(gate_proj, up_proj, packed)
    columns[1] = far(packed, "expert", 1)
    columns[2] = far(packed, "expert", 2)
    across[0] = swap(packed, "dp")
    wide_w = stage(gate_w, up_w)
    columns[0], columns[1], columns[2], across[0], wide_w = together(packed, columns[1], columns[2], across[0], wide_w)
    columns[3] = far(columns[0], "expert", 3)
    across[2] = swap(columns[2], "dp")
    across[1] = swap(columns[1], "dp")
    columns[3], across[1], across[2] = together(columns[3], across[1], across[2])
    across[3] = swap(columns[3], "dp")

    shards = [columns[2], across[2], columns[1], columns[0], across[1], across[0]]
    shards += [swap(shard, "sub") for shard in shards]
    keep, send, xe_0, diff_0, tall_w = expert_rows_chunk(
        "rows_0", shards, tok_count, top_count, expert_info, (wide_w, down_proj)
    )
    diff_0, columns[3], across[3] = together(diff_0, columns[3], across[3])
    send, across[3] = together(send, across[3])
    rows = tok_count
    paired_2 = keep[: 2 * rows] + swap(send[: 2 * rows], "sub").astype(F32)
    home_2 = paired_2[:rows] + swap(paired_2[rows:].astype(BF16), "dp").astype(F32)
    paired_10 = keep[2 * rows :] + swap(send[2 * rows :], "sub").astype(F32)
    away_1, away_0 = paired_10[2 * rows : 3 * rows].astype(BF16), paired_10[3 * rows :].astype(BF16)

    shards = [columns[3], across[3]]
    shards += [swap(shard, "sub") for shard in shards]
    keep, send, xe_3, diff_3 = expert_rows_chunk(
        "rows_3", shards, tok_count, top_count, expert_info, (wide_w, tall_w)
    )
    send, home_2 = together(send, home_2)
    back_2 = far(home_2.astype(BF16), "expert", 2)
    paired_3 = keep + swap(send, "sub").astype(F32)
    paired_3, away_1, diff_3 = together(paired_3, away_1, diff_3)
    home_3 = paired_3[:rows] + swap(paired_3[rows:].astype(BF16), "dp").astype(F32)
    gate_grads, up_grads, down_grads = weight_grads((xe_0, xe_3), (diff_0, diff_3))
    home_1 = paired_10[:rows] + swap(away_1, "dp").astype(F32)
    home_3, gate_grads = together(home_3, gate_grads)
    home_1, away_0 = together(home_1, away_0)
    back_3 = far(home_3.astype(BF16), "expert", 3)
    back_0 = swap(away_0, "dp")
    back_1 = far(home_1.astype(BF16), "expert", 1)
    arrived = (back_0, back_1, back_2, back_3)
    input_grad, routing_grad = finish(paired_10[rows : 2 * rows], arrived, routes)
    return (input_grad, routing_grad, gate_grads, up_grads, down_grads)


def expert_rows(inputs, gate_w, up_w, down_w):
    rows_x, rows_e = inputs
    leading = rows_x.shape[:-1]
    model_width = rows_x.shape[-1]
    hidden = gate_w.shape[1]
    flat_x = rows_x.reshape(-1, model_width)
    flat_e = rows_e.reshape(-1, model_width)
    contract = (((1,), (1,)), ((), ()))
    pre_gate = jnp.dot(flat_x, gate_w, preferred_element_type=jnp.float32)
    pre_up = jnp.dot(flat_x, up_w, preferred_element_type=jnp.float32)
    sigmoid_gate = jax.nn.sigmoid(pre_gate)
    silu_gate = pre_gate * sigmoid_gate
    hidden_act = silu_gate * pre_up
    hidden_low = hidden_act.astype(jnp.bfloat16)
    back_hidden = lax.dot_general(flat_e, down_w, contract, preferred_element_type=jnp.float32)
    product = jnp.sum(hidden_act * back_hidden, axis=1)
    silu_slope = sigmoid_gate * (1.0 + pre_gate * (1.0 - sigmoid_gate))
    diff_gate = (back_hidden * pre_up * silu_slope).astype(jnp.bfloat16)
    diff_up = (back_hidden * silu_gate).astype(jnp.bfloat16)
    row_grad = lax.dot_general(
        diff_gate, gate_w, contract, preferred_element_type=jnp.float32
    ) + lax.dot_general(diff_up, up_w, contract, preferred_element_type=jnp.float32)
    return (
        row_grad.reshape(leading + (model_width,)),
        product.reshape(leading),
        rows_x,
        rows_e,
        hidden_low.reshape(leading + (hidden,)),
        diff_gate.reshape(leading + (hidden,)),
        diff_up.reshape(leading + (hidden,)),
    )


def chosen_experts(layer_input, output_grad, routes, routing_weight, gate_proj, up_proj, down_proj):
    tok_count, model_width = layer_input.shape
    top_count = routes.shape[1]
    positions = lax.axis_size(("expert", "dp"))
    capacity = min(tok_count, 2 * tok_count * top_count // positions)
    row_count = tok_count * top_count
    slot_count = positions * capacity
    target = routes.reshape(-1)
    member = (target[:, None] == jnp.arange(positions, dtype=jnp.int32)[None, :]).astype(jnp.int32)
    earlier = jnp.cumsum(member, axis=0) - member
    slot_rank = jnp.sum(earlier * member, axis=1)
    slot_index = target * capacity + slot_rank
    source = (
        jnp.full((slot_count,), row_count, jnp.int32)
        .at[slot_index]
        .set(jnp.arange(row_count, dtype=jnp.int32))
    )
    filled = source < row_count
    picked = jnp.minimum(source, row_count - 1)
    token_index = picked // top_count
    row_scale = jnp.where(filled, routing_weight.reshape(-1)[picked], 0.0)
    send_x = jnp.where(
        filled[:, None], layer_input[token_index], jnp.zeros((), layer_input.dtype)
    ).reshape(positions, 1, capacity, model_width)
    send_e = (
        (row_scale[:, None] * output_grad[token_index].astype(jnp.float32))
        .astype(jnp.bfloat16)
        .reshape(positions, 1, capacity, model_width)
    )
    gate_w = gate_proj[0]
    up_w = up_proj[0]
    down_w = down_proj[0]
    hidden = gate_w.shape[1]
    paired = (
        lax.all_gather(send_x, "sub", axis=1, tiled=True),
        lax.all_gather(send_e, "sub", axis=1, tiled=True),
    )
    results = expert_rows(
        (
            lax.all_to_all(paired[0], ("expert", "dp"), split_axis=0, concat_axis=0, tiled=True),
            lax.all_to_all(paired[1], ("expert", "dp"), split_axis=0, concat_axis=0, tiled=True),
        ),
        gate_w,
        up_w,
        down_w,
    )
    row_part, product_part, rows_x, rows_e, hidden_low, diff_gate, diff_up = results
    returned = (
        lax.all_to_all(row_part, ("expert", "dp"), split_axis=0, concat_axis=0, tiled=True),
        lax.all_to_all(product_part, ("expert", "dp"), split_axis=0, concat_axis=0, tiled=True),
    )
    summed = (
        lax.psum_scatter(returned[0], "sub", scatter_dimension=1, tiled=True),
        lax.psum_scatter(returned[1], "sub", scatter_dimension=1, tiled=True),
    )
    back_rows = summed[0].astype(jnp.bfloat16)
    back_products = summed[1].astype(jnp.bfloat16)
    per_row = (
        back_rows.reshape(slot_count, model_width)[slot_index]
        .astype(jnp.float32)
        .reshape(tok_count, top_count, model_width)
    )
    input_grad = jnp.sum(per_row, axis=1).astype(jnp.bfloat16)
    routing_grad = (
        back_products.reshape(slot_count)[slot_index]
        .astype(jnp.float32)
        .reshape(tok_count, top_count)
        / routing_weight
    )
    over_rows = (((0,), (0,)), ((), ()))
    flat_x = rows_x.reshape(-1, model_width)
    flat_e = rows_e.reshape(-1, model_width)
    gate_grads = lax.dot_general(
        flat_x, diff_gate.reshape(-1, hidden), over_rows, preferred_element_type=jnp.float32
    ).astype(jnp.bfloat16)[None]
    up_grads = lax.dot_general(
        flat_x, diff_up.reshape(-1, hidden), over_rows, preferred_element_type=jnp.float32
    ).astype(jnp.bfloat16)[None]
    down_grads = lax.dot_general(
        hidden_low.reshape(-1, hidden), flat_e, over_rows, preferred_element_type=jnp.float32
    ).astype(jnp.bfloat16)[None]
    return (input_grad, routing_grad, gate_grads, up_grads, down_grads)


def per_device(layer_input, output_grad, routes, routing_weight, gate_proj, up_proj, down_proj):
    args = (layer_input, output_grad, routes, routing_weight, gate_proj, up_proj, down_proj)
    lines = lax.axis_size("expert")
    pairs = lax.axis_size("dp") == 2 and lax.axis_size("sub") == 2 and lines & (lines - 1) == 0
    fits = layer_input.shape[0] % FOLD == 0 and 2 * routes.shape[1] * layer_input.shape[0] <= FOLD * SIDE
    if fits and pairs and lines == 4 and 2 * lines == routes.shape[1] and gate_proj.shape[0] == 1:
        return every_token_to_every_expert(*args)
    return chosen_experts(*args)


def solution(mesh):
    placed = (
        P(("group", "expert", "dp", "sub"), None),
        P(("group", "expert", "dp", "sub"), None),
        P(("group", "expert", "dp", "sub"), None),
        P(("group", "expert", "dp", "sub"), None),
        P(("expert", "dp"), None, "sub"),
        P(("expert", "dp"), None, "sub"),
        P(("expert", "dp"), "sub", None),
    )
    return jax.shard_map(
        per_device,
        mesh=mesh,
        in_specs=placed,
        out_specs=(
            P(("group", "expert", "dp", "sub"), None),
            P(("group", "expert", "dp", "sub"), None),
            P(("group", "expert", "dp"), None, "sub"),
            P(("group", "expert", "dp"), None, "sub"),
            P(("group", "expert", "dp"), "sub", None),
        ),
        check_vma=False,
    )
```

```python
import functools

import jax
import jax.numpy as jnp
from jax import lax
from jax.experimental import pallas as pl
from jax.experimental.pallas import tpu as pltpu
from jax.sharding import PartitionSpec as P

F32 = jnp.float32
BF16 = jnp.bfloat16
SIDE = 128
FOLD = 16
NT = (((1,), (1,)), ((), ()))
TN = (((0,), (0,)), ((), ()))
MIB = 1024 * 1024


def split_columns(values, count, lane):
    high = values.astype(BF16)
    low = (values - high.astype(F32)).astype(BF16)
    zero = jnp.zeros_like(high)
    return jnp.where(lane < count, high, jnp.where(lane < 2 * count, low, zero))


def in_vmem(count):
    return [pl.BlockSpec(memory_space=pltpu.VMEM)] * count


def in_hbm(count):
    return [pl.BlockSpec(memory_space=pl.ANY)] * count


def held(*arrays):
    return [pltpu.with_memory_space_constraint(array, pltpu.VMEM) for array in arrays]


def left(*arrays):
    return [pltpu.with_memory_space_constraint(array, pltpu.HBM) for array in arrays]


def pack_kernel(x_ref, e_ref, routes_ref, weight_ref, out_ref, routes_held, weight_held, sems):
    tok_count, width = x_ref.shape
    top_count = routes_ref.shape[0]
    folds = tok_count // FOLD
    copies = [
        pltpu.make_async_copy(routes_ref, routes_held, sems.at[0]),
        pltpu.make_async_copy(weight_ref, weight_held, sems.at[1]),
    ]
    for i in range(2 * folds):
        source = (x_ref, e_ref)[i // folds].at[pl.ds(i % folds * FOLD, FOLD)]
        copies.append(pltpu.make_async_copy(source, out_ref.at[:, pl.ds(i * width, width)], sems.at[2 + i]))
    for copy in copies:
        copy.start()
    lane = lax.broadcasted_iota(jnp.int32, (FOLD, SIDE), 1)
    expert = lax.rem(lax.broadcasted_iota(jnp.int32, (SIDE, tok_count), 0), top_count)
    copies[0].wait()
    copies[1].wait()
    routes = routes_held[...]
    weight = weight_held[...]
    table = jnp.zeros((SIDE, tok_count), F32)
    for k in range(top_count):
        table += jnp.where(routes[k : k + 1, :] == expert, weight[k : k + 1, :], 0.0)
    table = table.T
    side = jnp.zeros((FOLD, SIDE), BF16)
    for i in range(folds):
        here = split_columns(table[i * FOLD : (i + 1) * FOLD], top_count, lane - 2 * i * top_count)
        side = jnp.where(lane < 2 * i * top_count, side, here)
    out_ref[:, 2 * folds * width :] = side
    for copy in copies[2:]:
        copy.wait()


def pack(x, e, routes, weight):
    tok_count, width = x.shape
    top_count = routes.shape[1]
    blocks = 2 * tok_count // FOLD
    return pl.pallas_call(
        pack_kernel,
        in_specs=in_hbm(4),
        out_specs=in_vmem(1)[0],
        out_shape=pltpu.VMEM((FOLD, blocks * width + SIDE), BF16),
        scratch_shapes=[
            pltpu.VMEM((top_count, tok_count), jnp.int32),
            pltpu.VMEM((top_count, tok_count), F32),
            pltpu.SemaphoreType.DMA((2 + blocks,)),
        ],
        compiler_params=pltpu.CompilerParams(vmem_limit_bytes=4 * MIB),
        name="pack_tokens",
    )(*left(x, e, routes.T, weight.T))


def stage_kernel(gate_ref, up_ref, wide_ref, sems):
    _, width, hidden = gate_ref.shape
    pieces = sems.shape[1]
    block = width // pieces
    copies = []
    for i in range(pieces):
        here = pl.ds(i * block, block)
        copies += [
            pltpu.make_async_copy(gate_ref.at[0, here], wide_ref.at[here, pl.ds(0, hidden)], sems.at[0, i]),
            pltpu.make_async_copy(up_ref.at[0, here], wide_ref.at[here, pl.ds(hidden, hidden)], sems.at[1, i]),
        ]
    for copy in copies:
        copy.start()
    for copy in copies:
        copy.wait()


def stage(gate_w, up_w):
    _, width, hidden = gate_w.shape
    return pl.pallas_call(
        stage_kernel,
        in_specs=in_hbm(2),
        out_specs=in_vmem(1)[0],
        out_shape=pltpu.VMEM((width, 2 * hidden), BF16),
        scratch_shapes=[pltpu.SemaphoreType.DMA((2, 4))],
        compiler_params=pltpu.CompilerParams(vmem_limit_bytes=8 * MIB),
        cost_estimate=pl.CostEstimate(flops=1, bytes_accessed=1, transcendentals=0),
        name="stage_weights",
    )(*left(gate_w, up_w))


def rows_kernel(shards, experts, first, expert_ref, *refs):
    shard_refs = refs[:shards]
    wide_ref, down_ref, keep_ref, send_ref, xe_ref, diff_ref = refs[shards : shards + 6]
    width = xe_ref.shape[1]
    rows = xe_ref.shape[0] // 2
    tok_count = rows // shards
    folds = tok_count // FOLD
    half = rows // 2
    hidden = diff_ref.shape[1] // 3
    chosen = expert_ref[:1, :] != 0
    lane = lax.broadcasted_iota(jnp.int32, (1, SIDE), 1)
    if first:
        tall_ref, table_ref, sems = refs[shards + 6 :]
        pieces = 4
        block = hidden // pieces
        copies = []
        for i, ref in enumerate(shard_refs):
            for j in range(folds):
                here = pl.ds(i * tok_count + j * FOLD, FOLD)
                copies.append((ref.at[:, pl.ds(j * width, width)], xe_ref.at[here]))
        count = len(copies)
        for i in range(pieces):
            here = pl.ds(i * block, block)
            copies.append((down_ref.at[0, here], tall_ref.at[here]))
        for i, ref in enumerate(shard_refs):
            for j in range(folds):
                here = pl.ds(rows + i * tok_count + j * FOLD, FOLD)
                copies.append((ref.at[:, pl.ds((folds + j) * width, width)], xe_ref.at[here]))
            copies.append((ref.at[:, pl.ds(2 * folds * width, SIDE)], table_ref.at[pl.ds(i * FOLD, FOLD)]))
        copies = [pltpu.make_async_copy(src, dst, sems.at[i]) for i, (src, dst) in enumerate(copies)]
        for copy in copies:
            copy.start()
        for copy in copies[:count]:
            copy.wait()
        pre = jnp.dot(xe_ref[:rows, :], wide_ref[...], preferred_element_type=F32)
        for copy in copies[count:]:
            copy.wait()
        e = xe_ref[rows:, :]
        table = table_ref[...].astype(F32)
    else:
        tall_ref = down_ref

        def pick(start):
            return jnp.concatenate(
                [ref[:, (start + j) * width : (start + j + 1) * width] for ref in shard_refs for j in range(folds)], axis=0
            )

        x, e = pick(0), pick(folds)
        xe_ref[:rows, :] = x
        xe_ref[rows:, :] = e
        pre = jnp.dot(x, wide_ref[...], preferred_element_type=F32)
        table = jnp.concatenate([ref[:, 2 * folds * width :] for ref in shard_refs], axis=0).astype(F32)
    weights = []
    for j in range(folds):
        mine = chosen & (lane >= 2 * j * experts) & (lane < 2 * (j + 1) * experts)
        weights.append(jnp.sum(jnp.where(mine, table, 0.0), axis=1, keepdims=True))
    weight = jnp.concatenate(
        [weights[j][i * FOLD : (i + 1) * FOLD] for i in range(shards) for j in range(folds)], axis=0
    )
    back = lax.dot_general(e, tall_ref[...], NT, preferred_element_type=F32)
    pre_gate, pre_up = pre[:, :hidden], pre[:, hidden:]
    sig = jax.nn.sigmoid(pre_gate)
    silu = pre_gate * sig
    act = silu * pre_up
    product = jnp.sum(act * back, axis=1, keepdims=True)
    back = back * weight
    diff_gate = (back * pre_up * (sig * (1.0 + pre_gate * (1.0 - sig)))).astype(BF16)
    diff_up = (back * silu).astype(BF16)
    diff = jnp.concatenate([diff_gate, diff_up], axis=1)
    diff_ref[:, : 2 * hidden] = diff
    diff_ref[:, 2 * hidden :] = (act * weight).astype(BF16)
    block = 512
    for c in range(0, width, block):
        part = lax.dot_general(diff, wide_ref[c : c + block, :], NT, preferred_element_type=F32)
        keep_ref[:, c : c + block] = part[:half]
        send_ref[:, c : c + block] = part[half:].astype(BF16)
    lane = lax.broadcasted_iota(jnp.int32, (rows, SIDE), 1)
    side = split_columns(jnp.where(chosen, product, 0.0), experts, lane)
    keep_ref[:, width:] = side[:half].astype(F32)
    send_ref[:, width:] = side[half:]


def expert_rows_chunk(name, shards, tok_count, experts, expert_info, weights):
    count = len(shards)
    first = weights[1].ndim == 3
    width = (shards[0].shape[1] - SIDE) * FOLD // (2 * tok_count)
    rows = count * tok_count
    hidden = weights[0].shape[1] // 2
    out_shape = [
        pltpu.VMEM((rows // 2, width + SIDE), F32),
        pltpu.VMEM((rows // 2, width + SIDE), BF16),
        pltpu.VMEM((2 * rows, width), BF16),
        pltpu.VMEM((rows, 3 * hidden), BF16),
    ]
    scratch_shapes = []
    if first:
        out_shape.append(pltpu.VMEM((hidden, width), BF16))
        scratch_shapes = [
            pltpu.VMEM((count * FOLD, SIDE), BF16),
            pltpu.SemaphoreType.DMA((count * (2 * tok_count // FOLD + 1) + 4,)),
        ]
    return pl.pallas_call(
        functools.partial(rows_kernel, count, experts, first),
        in_specs=in_vmem(1) + (in_hbm(count) + in_vmem(1) + in_hbm(1) if first else in_vmem(count + 2)),
        out_specs=in_vmem(len(out_shape)),
        out_shape=out_shape,
        scratch_shapes=scratch_shapes,
        compiler_params=pltpu.CompilerParams(vmem_limit_bytes=16 * MIB),
        cost_estimate=pl.CostEstimate(flops=1, bytes_accessed=1, transcendentals=0),
        name=name,
    )(expert_info, *(left(*shards) if first else shards), weights[0], *(left(weights[1]) if first else (weights[1],)))


def grads_kernel(parts, *refs):
    xe_refs = refs[:parts]
    diff_refs = refs[parts : 2 * parts]
    gate_out, up_out, down_out, both_ref, down_ref, out_sems = refs[2 * parts :]
    hidden = gate_out.shape[2]
    width = gate_out.shape[1]
    block = width // out_sems.shape[0]
    diffs = jnp.concatenate([ref[:, : 2 * hidden] for ref in diff_refs], axis=0)
    hidden_t = jnp.concatenate([ref[:, 2 * hidden :] for ref in diff_refs], axis=0).T
    leaving = []
    for i, c in enumerate(range(0, width, block)):
        columns = slice(c, c + block)
        here = pl.ds(c, block)
        x = jnp.concatenate([ref[: ref.shape[0] // 2, columns] for ref in xe_refs], axis=0)
        e = jnp.concatenate([ref[ref.shape[0] // 2 :, columns] for ref in xe_refs], axis=0)
        both_ref[columns, :] = lax.dot_general(x, diffs, TN, preferred_element_type=F32).astype(BF16)
        down_ref[:, columns] = jnp.dot(hidden_t, e, preferred_element_type=F32).astype(BF16)
        copies = [
            pltpu.make_async_copy(both_ref.at[here, pl.ds(0, hidden)], gate_out.at[0, here], out_sems.at[i, 0]),
            pltpu.make_async_copy(both_ref.at[here, pl.ds(hidden, hidden)], up_out.at[0, here], out_sems.at[i, 1]),
            pltpu.make_async_copy(down_ref.at[:, here], down_out.at[0, :, here], out_sems.at[i, 2]),
        ]
        for copy in copies:
            copy.start()
        leaving += copies
    for copy in leaving:
        copy.wait()


def weight_grads(xe_parts, diff_parts):
    count = len(xe_parts)
    width = xe_parts[0].shape[1]
    hidden = diff_parts[0].shape[1] // 3
    total = sum(part.shape[0] for part in diff_parts)
    return pl.pallas_call(
        functools.partial(grads_kernel, count),
        in_specs=in_vmem(2 * count),
        out_specs=in_hbm(3),
        out_shape=[
            jax.ShapeDtypeStruct((1, width, hidden), BF16),
            jax.ShapeDtypeStruct((1, width, hidden), BF16),
            jax.ShapeDtypeStruct((1, hidden, width), BF16),
        ],
        scratch_shapes=[
            pltpu.VMEM((width, 2 * hidden), BF16),
            pltpu.VMEM((hidden, width), BF16),
            pltpu.SemaphoreType.DMA((2, 3)),
        ],
        compiler_params=pltpu.CompilerParams(vmem_limit_bytes=24 * MIB),
        cost_estimate=pl.CostEstimate(
            flops=6 * total * width * hidden, bytes_accessed=4 * total * width + 6 * width * hidden, transcendentals=0
        ),
        name="weight_grads",
    )(*xe_parts, *diff_parts)


def finish_kernel(parts, own_ref, *refs):
    routes_ref, input_ref, routing_ref = refs[parts:]
    width = input_ref.shape[1]
    top_count = routes_ref.shape[0]
    total = own_ref[...]
    for ref in refs[:parts]:
        total = total + ref[...].astype(F32)
    input_ref[...] = total[:, :width].astype(BF16)
    side = total[:, width:].T
    products = side[:top_count] + side[top_count : 2 * top_count]
    routes = routes_ref[...]
    picked = jnp.zeros(routes.shape, F32)
    for e in range(top_count):
        picked += jnp.where(routes == e, products[e : e + 1, :], 0.0)
    routing_ref[...] = picked


def finish(own_sum, arrived, routes):
    tok_count, top_count = routes.shape
    width = own_sum.shape[1] - SIDE
    input_grad, routing_grad = pl.pallas_call(
        functools.partial(finish_kernel, len(arrived)),
        in_specs=in_vmem(2 + len(arrived)),
        out_specs=in_vmem(2),
        out_shape=[
            jax.ShapeDtypeStruct((tok_count, width), BF16),
            jax.ShapeDtypeStruct((top_count, tok_count), F32),
        ],
        compiler_params=pltpu.CompilerParams(vmem_limit_bytes=4 * MIB),
        name="finish",
    )(own_sum, *arrived, routes.T)
    return input_grad, routing_grad.T


def swap(value, axis):
    return lax.ppermute(value, axis, [(0, 1), (1, 0)])


def far(value, axis, distance):
    return lax.ppermute(value, axis, [(i, i ^ distance) for i in range(lax.axis_size(axis))])


def together(*values):
    return lax.optimization_barrier(values)


def every_token_to_every_expert(
    layer_input, output_grad, routes, routing_weight, gate_proj, up_proj, down_proj
):
    tok_count, width = layer_input.shape
    top_count = routes.shape[1]
    lines = lax.axis_size("expert")
    expert = lax.axis_index("expert") * lax.axis_size("dp") + lax.axis_index("dp")
    lane = lax.broadcasted_iota(jnp.int32, (8, SIDE), 1)
    expert_info = (lax.rem(lane, top_count) == expert).astype(jnp.int32)
    packed = pack(layer_input, output_grad, routes, routing_weight)
    columns, across = {}, {}
    gate_w, up_w, packed = together(gate_proj, up_proj, packed)
    columns[1] = far(packed, "expert", 1)
    columns[2] = far(packed, "expert", 2)
    across[0] = swap(packed, "dp")
    wide_w = stage(gate_w, up_w)
    columns[0], columns[1], columns[2], across[0], wide_w = together(packed, columns[1], columns[2], across[0], wide_w)
    columns[3] = far(columns[0], "expert", 3)
    across[2] = swap(columns[2], "dp")
    across[1] = far(across[0], "expert", 1)
    columns[3], across[2], across[1] = together(columns[3], across[2], across[1])
    across[3] = swap(columns[3], "dp")

    shards = [columns[2], across[2], columns[1], columns[0], across[1], across[0]]
    shards += [swap(shard, "sub") for shard in shards]
    keep, send, xe_0, diff_0, tall_w = expert_rows_chunk(
        "rows_0", shards, tok_count, top_count, expert_info, (wide_w, down_proj)
    )
    diff_0, columns[3], across[3] = together(diff_0, columns[3], across[3])
    send, across[3] = together(send, across[3])
    rows = tok_count
    paired_2 = keep[: 2 * rows] + swap(send[: 2 * rows], "sub").astype(F32)
    home_2 = paired_2[:rows] + swap(paired_2[rows:].astype(BF16), "dp").astype(F32)
    paired_10 = keep[2 * rows :] + swap(send[2 * rows :], "sub").astype(F32)
    away_1, away_0 = paired_10[2 * rows : 3 * rows].astype(BF16), paired_10[3 * rows :].astype(BF16)

    shards = [columns[3], across[3]]
    shards += [swap(shard, "sub") for shard in shards]
    keep, send, xe_3, diff_3 = expert_rows_chunk(
        "rows_3", shards, tok_count, top_count, expert_info, (wide_w, tall_w)
    )
    send, home_2 = together(send, home_2)
    back_2 = far(home_2.astype(BF16), "expert", 2)
    paired_3 = keep + swap(send, "sub").astype(F32)
    paired_3, away_1, diff_3 = together(paired_3, away_1, diff_3)
    home_3 = paired_3[:rows] + swap(paired_3[rows:].astype(BF16), "dp").astype(F32)
    gate_grads, up_grads, down_grads = weight_grads((xe_0, xe_3), (diff_0, diff_3))
    home_1 = paired_10[:rows] + swap(away_1, "dp").astype(F32)
    home_3, gate_grads, away_0 = together(home_3, gate_grads, away_0)
    back_0 = swap(away_0, "dp")
    back_3 = far(home_3.astype(BF16), "expert", 3)
    back_1 = far(home_1.astype(BF16), "expert", 1)
    arrived = (back_2, back_3, back_1, back_0)
    input_grad, routing_grad = finish(paired_10[rows : 2 * rows], arrived, routes)
    return (input_grad, routing_grad, gate_grads, up_grads, down_grads)


def expert_rows(inputs, gate_w, up_w, down_w):
    rows_x, rows_e = inputs
    leading = rows_x.shape[:-1]
    model_width = rows_x.shape[-1]
    hidden = gate_w.shape[1]
    flat_x = rows_x.reshape(-1, model_width)
    flat_e = rows_e.reshape(-1, model_width)
    contract = (((1,), (1,)), ((), ()))
    pre_gate = jnp.dot(flat_x, gate_w, preferred_element_type=jnp.float32)
    pre_up = jnp.dot(flat_x, up_w, preferred_element_type=jnp.float32)
    sigmoid_gate = jax.nn.sigmoid(pre_gate)
    silu_gate = pre_gate * sigmoid_gate
    hidden_act = silu_gate * pre_up
    hidden_low = hidden_act.astype(jnp.bfloat16)
    back_hidden = lax.dot_general(flat_e, down_w, contract, preferred_element_type=jnp.float32)
    product = jnp.sum(hidden_act * back_hidden, axis=1)
    silu_slope = sigmoid_gate * (1.0 + pre_gate * (1.0 - sigmoid_gate))
    diff_gate = (back_hidden * pre_up * silu_slope).astype(jnp.bfloat16)
    diff_up = (back_hidden * silu_gate).astype(jnp.bfloat16)
    row_grad = lax.dot_general(
        diff_gate, gate_w, contract, preferred_element_type=jnp.float32
    ) + lax.dot_general(diff_up, up_w, contract, preferred_element_type=jnp.float32)
    return (
        row_grad.reshape(leading + (model_width,)),
        product.reshape(leading),
        rows_x,
        rows_e,
        hidden_low.reshape(leading + (hidden,)),
        diff_gate.reshape(leading + (hidden,)),
        diff_up.reshape(leading + (hidden,)),
    )


def chosen_experts(layer_input, output_grad, routes, routing_weight, gate_proj, up_proj, down_proj):
    tok_count, model_width = layer_input.shape
    top_count = routes.shape[1]
    positions = lax.axis_size(("expert", "dp"))
    capacity = min(tok_count, 2 * tok_count * top_count // positions)
    row_count = tok_count * top_count
    slot_count = positions * capacity
    target = routes.reshape(-1)
    member = (target[:, None] == jnp.arange(positions, dtype=jnp.int32)[None, :]).astype(jnp.int32)
    earlier = jnp.cumsum(member, axis=0) - member
    slot_rank = jnp.sum(earlier * member, axis=1)
    slot_index = target * capacity + slot_rank
    source = (
        jnp.full((slot_count,), row_count, jnp.int32)
        .at[slot_index]
        .set(jnp.arange(row_count, dtype=jnp.int32))
    )
    filled = source < row_count
    picked = jnp.minimum(source, row_count - 1)
    token_index = picked // top_count
    row_scale = jnp.where(filled, routing_weight.reshape(-1)[picked], 0.0)
    send_x = jnp.where(
        filled[:, None], layer_input[token_index], jnp.zeros((), layer_input.dtype)
    ).reshape(positions, 1, capacity, model_width)
    send_e = (
        (row_scale[:, None] * output_grad[token_index].astype(jnp.float32))
        .astype(jnp.bfloat16)
        .reshape(positions, 1, capacity, model_width)
    )
    gate_w = gate_proj[0]
    up_w = up_proj[0]
    down_w = down_proj[0]
    hidden = gate_w.shape[1]
    paired = (
        lax.all_gather(send_x, "sub", axis=1, tiled=True),
        lax.all_gather(send_e, "sub", axis=1, tiled=True),
    )
    results = expert_rows(
        (
            lax.all_to_all(paired[0], ("expert", "dp"), split_axis=0, concat_axis=0, tiled=True),
            lax.all_to_all(paired[1], ("expert", "dp"), split_axis=0, concat_axis=0, tiled=True),
        ),
        gate_w,
        up_w,
        down_w,
    )
    row_part, product_part, rows_x, rows_e, hidden_low, diff_gate, diff_up = results
    returned = (
        lax.all_to_all(row_part, ("expert", "dp"), split_axis=0, concat_axis=0, tiled=True),
        lax.all_to_all(product_part, ("expert", "dp"), split_axis=0, concat_axis=0, tiled=True),
    )
    summed = (
        lax.psum_scatter(returned[0], "sub", scatter_dimension=1, tiled=True),
        lax.psum_scatter(returned[1], "sub", scatter_dimension=1, tiled=True),
    )
    back_rows = summed[0].astype(jnp.bfloat16)
    back_products = summed[1].astype(jnp.bfloat16)
    per_row = (
        back_rows.reshape(slot_count, model_width)[slot_index]
        .astype(jnp.float32)
        .reshape(tok_count, top_count, model_width)
    )
    input_grad = jnp.sum(per_row, axis=1).astype(jnp.bfloat16)
    routing_grad = (
        back_products.reshape(slot_count)[slot_index]
        .astype(jnp.float32)
        .reshape(tok_count, top_count)
        / routing_weight
    )
    over_rows = (((0,), (0,)), ((), ()))
    flat_x = rows_x.reshape(-1, model_width)
    flat_e = rows_e.reshape(-1, model_width)
    gate_grads = lax.dot_general(
        flat_x, diff_gate.reshape(-1, hidden), over_rows, preferred_element_type=jnp.float32
    ).astype(jnp.bfloat16)[None]
    up_grads = lax.dot_general(
        flat_x, diff_up.reshape(-1, hidden), over_rows, preferred_element_type=jnp.float32
    ).astype(jnp.bfloat16)[None]
    down_grads = lax.dot_general(
        hidden_low.reshape(-1, hidden), flat_e, over_rows, preferred_element_type=jnp.float32
    ).astype(jnp.bfloat16)[None]
    return (input_grad, routing_grad, gate_grads, up_grads, down_grads)


def per_device(layer_input, output_grad, routes, routing_weight, gate_proj, up_proj, down_proj):
    args = (layer_input, output_grad, routes, routing_weight, gate_proj, up_proj, down_proj)
    lines = lax.axis_size("expert")
    pairs = lax.axis_size("dp") == 2 and lax.axis_size("sub") == 2 and lines & (lines - 1) == 0
    fits = layer_input.shape[0] % FOLD == 0 and 2 * routes.shape[1] * layer_input.shape[0] <= FOLD * SIDE
    if fits and pairs and lines == 4 and 2 * lines == routes.shape[1] and gate_proj.shape[0] == 1:
        return every_token_to_every_expert(*args)
    return chosen_experts(*args)


def solution(mesh):
    placed = (
        P(("group", "expert", "dp", "sub"), None),
        P(("group", "expert", "dp", "sub"), None),
        P(("group", "expert", "dp", "sub"), None),
        P(("group", "expert", "dp", "sub"), None),
        P(("expert", "dp"), None, "sub"),
        P(("expert", "dp"), None, "sub"),
        P(("expert", "dp"), "sub", None),
    )
    return jax.shard_map(
        per_device,
        mesh=mesh,
        in_specs=placed,
        out_specs=(
            P(("group", "expert", "dp", "sub"), None),
            P(("group", "expert", "dp", "sub"), None),
            P(("group", "expert", "dp"), None, "sub"),
            P(("group", "expert", "dp"), None, "sub"),
            P(("group", "expert", "dp"), "sub", None),
        ),
        check_vma=False,
    )
```
